32 devices in a mesh: dp: 16 (over z, x, core), ctx: 2 (over y).
Axes of the slice: x: 2, y: 2, z: 4, core: 2. Of those that a mesh axis runs over, the one named last changes fastest.
Arguments:
- hidden_in: bfloat16 [16, 256, 2688], P('dp', 'ctx'), may hold values from -0.08984375 to 0.08984375
- queries: bfloat16 [16, 256, 2048], P('dp', 'ctx'), may hold values from -60 to 60
- key_states: bfloat16 [16, 256, 1024], P('dp', 'ctx'), may hold values from -4 to 4
- value_states: bfloat16 [16, 256, 1024], P('dp', 'ctx'), may hold values from -6 to 6
- out_grad: bfloat16 [16, 256, 2048], P('dp', 'ctx'), may hold values from -48 to 48
- segment_ids: int32 [16, 256], P('dp', 'ctx'), may hold values from 0 to 3, never falling along the last dimension, each value on 1 to 128 neighbouring positions
Outputs:
- query_grad: bfloat16 [16, 256, 2048], P('dp', 'ctx')
- key_grad: bfloat16 [16, 256, 1024], P('dp', 'ctx')
- value_grad: bfloat16 [16, 256, 1024], P('dp', 'ctx')
- weight_grad: float32 [2688, 2048], P('dp', 'ctx')
The draws below stay inside these ranges and needn't reach their ends.
Inputs may be any that keep to these rules, and one draw needn't show every extreme that they name: `segment_ids`: documents of a trace are numbered in order of position.
All inputs are finite; a program needn't handle non-finite values.
Results may differ from the reference program's by a relative error of at most 0.0096.
Values may be sent and summed in bfloat16 or wider, within the bound.
No kernel may reach another device: no remote copies, remote signals or barrier semaphores. Data moves between devices by JAX's collectives and lax.ppermute only.
A program may use at most 128 MiB of HBM per device.

```python
import math
import jax
import jax.numpy as jnp
import numpy as np
from jax import lax

QH = 16
KVH = 8
HD = 128
DW = 2688
WIN = 1024
SEGS = 4
TOK_DEV = 128
SEQ = 256
TRACES = 16
HOPS = 1


def draw_pair(key):
    base_key = jax.random.fold_in(key, 4242)
    query_key, keys_key = jax.random.split(base_key, 2)
    query_shape = (TRACES, SEQ, QH * HD)
    key_shape = (TRACES, SEQ, KVH * HD)
    query_vals = jnp.clip(jax.random.normal(query_key, query_shape, jnp.float32), -4.0, 4.0)
    key_vals = jnp.clip(jax.random.normal(keys_key, key_shape, jnp.float32), -4.0, 4.0)
    return (query_vals, key_vals)


def draw_queries(key, part):
    return draw_pair(key)[0].astype(jnp.bfloat16)


def draw_key_states(key, part):
    return draw_pair(key)[1].astype(jnp.bfloat16)


def with_spikes(result, stream_key, source, target, shards_of, factor):
    def block_of(position):
        return (jnp.arange(result.shape[position]) // (result.shape[position] // shards_of)).reshape((-1,) + (1,) * (result.ndim - 1 - position))

    one_side = jax.random.permutation(stream_key, shards_of)[block_of(target)]
    other_side = (block_of(target) + shards_of // 2) % shards_of
    return jnp.where((block_of(source) == one_side) | (block_of(source) == other_side), factor * result, result)


def shard_levels(key, dims, pieces, smallest, high):
    def one(dim, parts):
        draws = jax.random.uniform(jax.random.fold_in(jax.random.fold_in(key, 6), dim), (parts,), jnp.float32, smallest / len(pieces), high / len(pieces))
        return jnp.repeat(jnp.exp(draws), dims[dim] // parts).reshape((-1,) + (1,) * (len(dims) - dim - 1))

    factor_of = one(*pieces[0])
    for cut in pieces[1:]:
        factor_of = factor_of * one(*cut)
    return factor_of


def split_up(count, total, limit, slope):
    portions = [(1 << 20) // math.isqrt(standing ** slope) + 1 for standing in range(2, count + 1)]
    spare, counts = total - limit - (count - 1), [1] * (count - 1)
    while spare > 0:
        free = [i for i in range(count - 1) if counts[i] < limit]
        mass, remaining = sum([portions[i] for i in free]), spare
        for i in free:
            extra = min(limit - counts[i], max(1, remaining * portions[i] // mass), spare)
            counts[i] = counts[i] + extra
            spare = spare - extra
    return np.array([limit] + counts)


def uneven_parts(rng, count, total, reach, lean):
    if count == 2:
        one = jax.random.randint(rng, (), max(1, total - reach), min(reach, total - 1) + 1)
        return jnp.stack([one, total - one])
    sizes = jnp.asarray(split_up(count, total, reach, lean), jnp.int32)
    twos = (count - 1) // 2
    donor, receiver = sizes[1:1 + 2 * twos:2], sizes[2:2 + 2 * twos:2]
    margin = jnp.minimum(donor - 1, reach - receiver)
    moved = jax.random.randint(jax.random.fold_in(rng, 1), (twos,), 0, 1 << 20) % (margin + 1)
    sizes = sizes.at[1:1 + 2 * twos:2].set(donor - moved).at[2:2 + 2 * twos:2].set(receiver + moved)
    return sizes[jax.random.permutation(jax.random.fold_in(rng, 2), count)]


def noise(own_key, shape, deviation, limit, pieces=(), kind=jnp.bfloat16):
    level = shard_levels(own_key, shape, pieces, -0.22, 0.18) if pieces else 1.0
    values = jax.random.normal(own_key, shape, jnp.float32) * deviation * level
    return jnp.minimum(jnp.maximum(values, -limit), limit).astype(kind)


def bell_draw_with(stream_key, dims, deviation, limit, shards, heavy, kind=jnp.bfloat16):
    drawn = deviation * jax.random.normal(stream_key, dims, jnp.float32)
    if shards:
        drawn = drawn * shard_levels(stream_key, dims, shards, -0.22, 0.18)
    return jnp.clip(with_spikes(drawn, jax.random.fold_in(stream_key, 3), *heavy), -limit, limit).astype(kind)


def setup_inputs(seed: int = 0) -> dict:
    keys = jax.random.split(jax.random.key(seed), 7)
    hidden_in = bell_draw_with(keys[0], (TRACES, SEQ, DW), 0.015, 0.08984375, ((0, 16), (1, 2)), (0, 2, 16, 2.0))
    queries = draw_queries(jax.random.fold_in(keys[6], 71), 0)
    key_states = draw_key_states(jax.random.fold_in(keys[6], 71), 0)
    value_states = noise(keys[3], (TRACES, SEQ, KVH * HD), 1.0, 6.0, ((0, 16), (1, 2)))
    out_grad = noise(keys[4], (TRACES, SEQ, QH * HD), 8.0, 48.0, ((0, 16), (1, 2)))
    segment_ids = jax.vmap(lambda own: jnp.searchsorted(jnp.cumsum(uneven_parts(own, SEGS, SEQ, SEQ // 2, 1)), jnp.arange(SEQ), side="right"))(jax.random.split(keys[5], TRACES)).reshape((TRACES, SEQ)).astype(jnp.int32)
    return {"hidden_in": hidden_in, "queries": queries, "key_states": key_states, "value_states": value_states, "out_grad": out_grad, "segment_ids": segment_ids}


SCORE_FLOOR = -1e30


def round_keep(values_in):
    return lax.optimization_barrier(values_in.astype(jnp.bfloat16)).astype(jnp.float32)


def one_trace(queries, key_states, value_states, out_grad, segment_ids):
    score_scale = HD ** -0.5
    group_size = QH // KVH
    rim_span = HOPS * TOK_DEV
    key_span = rim_span + TOK_DEV
    keys_padded = jnp.pad(key_states, ((rim_span, 0), (0, 0)))
    values_padded = jnp.pad(value_states, ((rim_span, 0), (0, 0)))
    segs_padded = jnp.pad(segment_ids, (rim_span, 0), constant_values=-1)

    def block_step(carried, block_index):
        key_total, value_total = carried
        first_row = (block_index * TOK_DEV).astype(jnp.int32)
        query_block = lax.dynamic_slice_in_dim(queries, first_row, TOK_DEV, 0).reshape(TOK_DEV, KVH, group_size, HD).astype(jnp.float32)
        grad_block = lax.dynamic_slice_in_dim(out_grad, first_row, TOK_DEV, 0).reshape(TOK_DEV, KVH, group_size, HD).astype(jnp.float32)
        key_block = lax.dynamic_slice_in_dim(keys_padded, first_row, key_span, 0).reshape(key_span, KVH, HD).astype(jnp.float32)
        value_block = lax.dynamic_slice_in_dim(values_padded, first_row, key_span, 0).reshape(key_span, KVH, HD).astype(jnp.float32)
        query_segs = lax.dynamic_slice_in_dim(segment_ids, first_row, TOK_DEV, 0)
        key_segs = lax.dynamic_slice_in_dim(segs_padded, first_row, key_span, 0)
        query_pos = first_row + jnp.arange(TOK_DEV, dtype=jnp.int32)
        key_pos = first_row - rim_span + jnp.arange(key_span, dtype=jnp.int32)
        distance = query_pos[:, None] - key_pos[None, :]
        allowed = (key_pos[None, :] >= 0) & (distance >= 0) & (distance < WIN) & (query_segs[:, None] == key_segs[None, :])
        scores = jnp.einsum("ikgd,jkd->kgij", query_block, key_block) * score_scale
        scores = jnp.where(allowed[None, None], scores, SCORE_FLOOR)
        row_peak = jnp.max(scores, axis=3, keepdims=True)
        weights = jnp.where(allowed[None, None], jnp.exp(scores - row_peak), 0.0)
        probs_full = weights / jnp.sum(weights, axis=3, keepdims=True)
        probs_low = round_keep(probs_full)
        attn_out = jnp.einsum("kgij,jkd->kgid", probs_low, value_block)
        row_delta = jnp.einsum("ikgd,kgid->kgi", grad_block, attn_out)
        dprobs = jnp.einsum("ikgd,jkd->kgij", grad_block, value_block)
        dscores = round_keep(probs_full * (dprobs - row_delta[..., None]))
        query_part = (jnp.einsum("kgij,jkd->ikgd", dscores, key_block) * score_scale).astype(jnp.bfloat16)
        key_part = round_keep(jnp.einsum("kgij,ikgd->jkd", dscores, query_block) * score_scale).reshape(key_span, KVH * HD)
        value_part = round_keep(jnp.einsum("kgij,ikgd->jkd", probs_low, grad_block)).reshape(key_span, KVH * HD)
        key_total = lax.dynamic_update_slice_in_dim(key_total, lax.dynamic_slice_in_dim(key_total, first_row, key_span, 0) + key_part, first_row, 0)
        value_total = lax.dynamic_update_slice_in_dim(value_total, lax.dynamic_slice_in_dim(value_total, first_row, key_span, 0) + value_part, first_row, 0)
        return (key_total, value_total), query_part.reshape(TOK_DEV, QH * HD)

    zeros_init = jnp.zeros((SEQ + rim_span, KVH * HD), jnp.float32)
    (key_total, value_total), query_blocks = lax.scan(block_step, (zeros_init, zeros_init), jnp.arange(SEQ // TOK_DEV, dtype=jnp.int32))
    key_grad = key_total[rim_span:].astype(jnp.bfloat16)
    value_grad = value_total[rim_span:].astype(jnp.bfloat16)
    return query_blocks.reshape(SEQ, QH * HD), key_grad, value_grad


def reference(hidden_in, queries, key_states, value_states, out_grad, segment_ids):
    def trace_step(grad_total, items):
        features, query_one, key_one, value_one, grad_one, segs_one = items
        query_grad, key_grad, value_grad = one_trace(query_one, key_one, value_one, grad_one, segs_one)
        both_grads = jnp.concatenate([key_grad, value_grad], axis=1)
        grad_total = grad_total + jnp.dot(features.T, both_grads, preferred_element_type=jnp.float32)
        return grad_total, (query_grad, key_grad, value_grad)

    start_total = jnp.zeros((DW, 2 * KVH * HD), jnp.float32)
    weight_grad, outputs = lax.scan(trace_step, start_total, (hidden_in, queries, key_states, value_states, out_grad, segment_ids))
    return outputs[0], outputs[1], outputs[2], weight_grad
```

```python
from functools import partial

import jax
import jax.numpy as jnp
from jax import lax
from jax.experimental import pallas as pl
from jax.experimental.pallas import tpu as pltpu
from jax.sharding import PartitionSpec as P

HD = 128
WIN = 1024
CHUNKS = 2
SCORE_FLOOR = -1e30
MIB = 1024 * 1024

NT = (((1,), (1,)), ((), ()))
TN = (((0,), (0,)), ((), ()))


def dot_f32(left, right, dims=(((1,), (0,)), ((), ()))):
    return lax.dot_general(left, right, dims, preferred_element_type=jnp.float32)


def shifted(value, axis, steps):
    count = lax.axis_size(axis)
    leading, last = (max(0, -steps), min(count, count - steps))
    return lax.ppermute(value, axis, [(source, source + steps) for source in range(leading, last)])


def attention_kernel(hops, group, place_ref, *refs):
    segs_ref, query_ref, grad_ref, key_ref, value_ref = refs[:5]
    rim_refs = refs[5 : 5 + 2 * hops]
    rim_segs = rim_refs[hops:]
    rim_pairs = rim_refs[:hops]
    outs = refs[5 + 2 * hops :]
    tok = query_ref.shape[0]
    heads = key_ref.shape[1] // HD
    rim = hops * tok
    span = rim + tok
    place = place_ref[0]
    scale = HD**-0.5

    query_segs = segs_ref[...].astype(jnp.float32)
    key_cols = [
        jnp.transpose(jnp.broadcast_to(ref[...].astype(jnp.float32), (tok, tok)))
        for ref in (*rim_segs, segs_ref)
    ]
    key_segs = jnp.concatenate(key_cols, axis=0)
    key_at = lax.broadcasted_iota(jnp.int32, (span, tok), 0)
    distance = rim + lax.broadcasted_iota(jnp.int32, (span, tok), 1) - key_at
    allowed = (
        (key_at >= rim - place * tok)
        & (distance >= 0)
        & (distance < WIN)
        & (key_segs == query_segs)
    )
    floor = jnp.where(allowed, 0.0, SCORE_FLOOR)
    floor = jnp.concatenate([floor] * group, axis=1)
    keep = floor == 0.0

    for head in range(heads):
        cols = slice(head * HD, (head + 1) * HD)
        value_cols = slice((heads + head) * HD, (heads + head + 1) * HD)
        q_cols = [slice((head * group + g) * HD, (head * group + g + 1) * HD) for g in range(group)]
        query = jnp.concatenate([query_ref[:, c] for c in q_cols], axis=0)
        grad = jnp.concatenate([grad_ref[:, c] for c in q_cols], axis=0)
        keys = jnp.concatenate([ref[:, cols] for ref in rim_pairs] + [key_ref[:, cols]], axis=0)
        values = jnp.concatenate(
            [ref[:, value_cols] for ref in rim_pairs] + [value_ref[:, cols]], axis=0
        )
        scores = jnp.where(keep, dot_f32(keys, query, NT) * scale, SCORE_FLOOR)
        weights = jnp.exp(scores - jnp.max(scores, axis=0, keepdims=True))
        probs = weights * (1.0 / jnp.sum(weights, axis=0, keepdims=True))
        probs_low = probs.astype(jnp.bfloat16)
        dprobs = dot_f32(values, grad, NT)
        delta = jnp.sum(probs_low.astype(jnp.float32) * dprobs, axis=0, keepdims=True)
        dscores = (probs * (dprobs - delta)).astype(jnp.bfloat16)
        query_part = (dot_f32(dscores, keys, TN) * scale).astype(jnp.bfloat16)
        for g, c in enumerate(q_cols):
            outs[0][:, c] = query_part[g * tok : (g + 1) * tok]
        key_part = dot_f32(dscores, query) * scale
        value_part = dot_f32(probs_low, grad)
        if hops == 1:
            first = place == 0
            key_rim, key_own = key_part[:tok], key_part[tok:]
            value_rim, value_own = value_part[:tok], value_part[tok:]
            outs[1][:, cols] = jnp.where(first, value_own, key_rim).astype(jnp.bfloat16)
            outs[2][:, cols] = jnp.where(first, key_own, value_rim).astype(jnp.bfloat16)
            outs[3][:, cols] = key_own.astype(jnp.bfloat16)
            outs[4][:, cols] = value_own.astype(jnp.bfloat16)
            outs[5][:, cols] = value_rim.astype(jnp.bfloat16)
        else:
            outs[1][:, cols] = key_part.astype(jnp.bfloat16)
            outs[2][:, cols] = value_part.astype(jnp.bfloat16)


def attend(chunk, place, segs, queries, out_grad, keys, values, rim_pairs, rim_segs):
    hops = len(rim_pairs)
    tok = queries.shape[0]
    group = queries.shape[1] // keys.shape[1]
    width = keys.shape[1] // CHUNKS
    heads = width // HD
    span = (hops + 1) * tok
    whole = lambda *shape: pl.BlockSpec(shape, lambda i, *_: (0,) * len(shape))
    part = lambda *shape: pl.BlockSpec(shape, lambda i, *_: (0, chunk))
    shape_of = lambda *shape: jax.ShapeDtypeStruct(shape, jnp.bfloat16)
    if hops == 1:
        out_shapes = [(tok, width)] * 5
    else:
        out_shapes = [(span, width)] * 2
    out_shapes = [(tok, group * width)] + out_shapes
    return pl.pallas_call(
        partial(attention_kernel, hops, group),
        grid_spec=pltpu.PrefetchScalarGridSpec(
            num_scalar_prefetch=1,
            grid=(1,),
            in_specs=[
                whole(1, tok),
                part(tok, group * width),
                part(tok, group * width),
                part(tok, width),
                part(tok, width),
            ]
            + [whole(tok, 2 * width)] * hops
            + [whole(1, tok)] * hops,
            out_specs=[whole(*shape) for shape in out_shapes],
        ),
        out_shape=[shape_of(*shape) for shape in out_shapes],
        compiler_params=pltpu.CompilerParams(vmem_limit_bytes=48 * MIB),
        cost_estimate=pl.CostEstimate(
            flops=heads * group * tok * span * HD * 10,
            bytes_accessed=16 * tok * width,
            transcendentals=heads * group * tok * span,
        ),
    )(place, segs, queries, out_grad, keys, values, *rim_pairs, *rim_segs)


def product_kernel(traces, *refs):
    own_ref, other_ref = refs[:2]
    grad_refs = refs[2 : 2 + traces]
    send_ref, keep_ref = refs[2 + traces :]
    features = jnp.concatenate(
        [ref[t] for t in range(traces) for ref in (own_ref, other_ref)], axis=1
    )
    grads = jnp.concatenate([ref[...] for ref in grad_refs], axis=0)
    half = features.shape[0] // 2
    send_ref[...] = dot_f32(features[:half], grads).astype(jnp.bfloat16)
    keep_ref[...] = dot_f32(features[half:], grads)


def product(own_features, other_features, grads):
    traces, rows, tok = own_features.shape
    width = grads[0].shape[1]
    return pl.pallas_call(
        partial(product_kernel, traces),
        out_shape=[
            jax.ShapeDtypeStruct((rows // 2, width), jnp.bfloat16),
            jax.ShapeDtypeStruct((rows // 2, width), jnp.float32),
        ],
        compiler_params=pltpu.CompilerParams(vmem_limit_bytes=48 * MIB),
        cost_estimate=pl.CostEstimate(
            flops=4 * traces * tok * rows * width,
            bytes_accessed=4 * traces * tok * (rows + width) + 3 * rows * width,
            transcendentals=0,
        ),
    )(own_features, other_features, *grads)


def local(hidden_in, queries, key_states, value_states, out_grad, segment_ids):
    tok = queries.shape[1]
    key_width = key_states.shape[2]
    width = key_width // CHUNKS
    ctx_count = lax.axis_size("ctx")
    hops = min(WIN // tok, ctx_count - 1)
    place = lax.axis_index("ctx")
    first = place == 0
    place_arg = place.astype(jnp.int32).reshape(1)

    dp_count = lax.axis_size("dp")
    slow_count, core_count = 4, 2
    mid_count = dp_count // (slow_count * core_count)
    dp_place = lax.axis_index("dp")
    core_at = dp_place % core_count
    mid_at = dp_place // core_count % mid_count
    slow_at = dp_place // (core_count * mid_count)

    def dp_send(value, move):
        pairs = []
        for source in range(dp_count):
            core = source % core_count
            mid = source // core_count % mid_count
            slow = source // (core_count * mid_count)
            slow, mid, core = move(slow, mid, core)
            pairs.append((source, (slow * mid_count + mid) * core_count + core))
        return lax.ppermute(value, "dp", pairs)

    swap_core = lambda slow, mid, core: (slow, mid, core ^ 1)
    mid_by = lambda step: lambda slow, mid, core: (slow, (mid + step) % mid_count, core)
    flip_slow = lambda bit: lambda slow, mid, core: (slow ^ bit, mid, core)
    swap_ctx = [(c, c ^ 1) for c in range(ctx_count)]

    own_keys, own_values = key_states[0], value_states[0]

    steps = range(hops, 0, -1)
    rim_pairs = []
    for chunk in range(CHUNKS):
        cols = slice(chunk * width, (chunk + 1) * width)
        pair = jnp.concatenate([own_keys[:, cols], own_values[:, cols]], axis=1)
        rim_pairs.append([shifted(pair, "ctx", step) for step in steps])
    rim_segs = [shifted(segment_ids, "ctx", step) for step in steps]

    rows = hidden_in.shape[2] // dp_count
    by_feature = hidden_in[0].T.reshape(slow_count, mid_count, core_count, rows, tok)
    order = (3, 1, 2, 0)
    by_feature = jnp.stack(
        [lax.dynamic_index_in_dim(by_feature, slow_at ^ flip, 0, False) for flip in order], axis=2
    )
    core_block = lambda at: lax.dynamic_index_in_dim(by_feature, at, 1, False)
    features = jnp.stack([core_block(core_at), dp_send(core_block(1 - core_at), swap_core)], axis=1)
    mid_block = lambda at: lax.dynamic_index_in_dim(features, at % mid_count, 0, False)
    features = jnp.concatenate(
        [mid_block(mid_at)]
        + [dp_send(mid_block(mid_at + step), mid_by(step)) for step in range(1, mid_count)],
        axis=0,
    )
    features = features.reshape(core_count * mid_count, slow_count * rows, tok)

    attended = [
        attend(
            chunk,
            place_arg,
            segment_ids,
            queries[0],
            out_grad[0],
            own_keys,
            own_values,
            rim_pairs[chunk],
            rim_segs,
        )
        for chunk in range(CHUNKS)
    ]
    query_grad = jnp.concatenate([outs[0] for outs in attended], axis=1)

    if ctx_count == 2:
        other_features = lax.ppermute(features, "ctx", swap_ctx)
        key_grads, value_grads, columns = [], [], []
        for _, sent, addend, key_own, value_own, value_rim in attended:
            late_keys = lax.ppermute(key_own, "ctx", [(1, 0)])
            arrived = lax.ppermute(sent, "ctx", swap_ctx)
            total = (addend.astype(jnp.float32) + arrived.astype(jnp.float32)).astype(jnp.bfloat16)
            columns.append(
                jnp.concatenate(
                    [jnp.where(first, total, value_own), jnp.where(first, late_keys, total)], axis=0
                )
            )
            key_grads.append(jnp.where(first, total, key_own))
            returned = lax.ppermute(value_rim, "ctx", [(1, 0)])
            value_grads.append(
                (value_own.astype(jnp.float32) + returned.astype(jnp.float32)).astype(jnp.bfloat16)
            )
        key_grad = jnp.concatenate(key_grads, axis=1)
        value_grad = jnp.concatenate(value_grads, axis=1)
    else:
        key_rows = jnp.concatenate([outs[1] for outs in attended], axis=1)
        value_rows = jnp.concatenate([outs[2] for outs in attended], axis=1)
        totals = [part[hops * tok :].astype(jnp.float32) for part in (key_rows, value_rows)]
        for step in range(1, hops + 1):
            low = (hops - step) * tok
            totals = [
                total + shifted(part[low : low + tok], "ctx", -step).astype(jnp.float32)
                for total, part in zip(totals, (key_rows, value_rows))
            ]
        key_grad, value_grad = (total.astype(jnp.bfloat16) for total in totals)
        both = lax.all_to_all(
            jnp.concatenate([key_grad, value_grad], axis=1),
            "ctx",
            split_axis=1,
            concat_axis=0,
            tiled=True,
        )
        columns = jnp.split(both, CHUNKS, axis=1)
        every = lax.all_gather(features, "ctx", axis=2, tiled=True)
        features, other_features = jnp.split(every, 2, axis=2)

    weight_parts = []
    for block in columns:
        near = [block] + [dp_send(block, mid_by(step)) for step in range(1, mid_count)]
        grads = [piece for held in near for piece in (held, dp_send(held, swap_core))]
        sent, kept = product(features, other_features, grads)
        half = kept + dp_send(sent, flip_slow(1)).astype(jnp.float32)
        last = dp_send(half[:rows].astype(jnp.bfloat16), flip_slow(2))
        weight_parts.append(half[rows:] + last.astype(jnp.float32))
    weight_grad = jnp.concatenate(weight_parts, axis=1)
    return (query_grad[None], key_grad[None], value_grad[None], weight_grad)


def solution(mesh):
    placed = (
        P("dp", "ctx", None),
        P("dp", "ctx", None),
        P("dp", "ctx", None),
        P("dp", "ctx", None),
        P("dp", "ctx", None),
        P("dp", "ctx"),
    )
    return jax.shard_map(
        local,
        mesh=mesh,
        in_specs=placed,
        out_specs=(
            P("dp", "ctx", None),
            P("dp", "ctx", None),
            P("dp", "ctx", None),
            P("dp", "ctx"),
        ),
        check_vma=False,
    )
```

```python
from functools import partial

import jax
import jax.numpy as jnp
from jax import lax
from jax.experimental import pallas as pl
from jax.experimental.pallas import tpu as pltpu
from jax.sharding import PartitionSpec as P

HD = 128
WIN = 1024
CHUNKS = 2
SCORE_FLOOR = -1e30
MIB = 1024 * 1024
SEG_ROWS = 16
SMALL = pl.CostEstimate(flops=1024, bytes_accessed=1024, transcendentals=0)

NT = (((1,), (1,)), ((), ()))
TN = (((0,), (0,)), ((), ()))


def dot_f32(left, right, dims=(((1,), (0,)), ((), ()))):
    return lax.dot_general(left, right, dims, preferred_element_type=jnp.float32)


def shifted(value, axis, steps):
    count = lax.axis_size(axis)
    leading, last = (max(0, -steps), min(count, count - steps))
    return lax.ppermute(value, axis, [(source, source + steps) for source in range(leading, last)])


def attention_kernel(hops, group, outs_count, place_ref, *refs):
    segs_ref, query_ref, grad_ref, key_ref, value_ref = refs[:5]
    rim_refs = refs[5 : 5 + 2 * hops]
    rim_segs = rim_refs[hops:]
    rim_pairs = rim_refs[:hops]
    outs = refs[-outs_count:]
    tok = query_ref.shape[0]
    heads = key_ref.shape[1] // HD
    rim = hops * tok
    span = rim + tok
    place = place_ref[0]
    scale = HD**-0.5

    query_segs = segs_ref[...].astype(jnp.float32)
    key_cols = [
        jnp.transpose(jnp.broadcast_to(ref[...].astype(jnp.float32)[:1], (tok, tok)))
        for ref in (*rim_segs, segs_ref)
    ]
    key_segs = jnp.concatenate(key_cols, axis=0)
    key_at = lax.broadcasted_iota(jnp.int32, (span, tok), 0)
    distance = rim + lax.broadcasted_iota(jnp.int32, (span, tok), 1) - key_at
    allowed = (
        (key_at >= rim - place * tok)
        & (distance >= 0)
        & (distance < WIN)
        & (key_segs == query_segs)
    )
    floor = jnp.where(allowed, 0.0, SCORE_FLOOR)
    floor = jnp.concatenate([floor] * group, axis=1)
    keep = floor == 0.0

    for head in range(heads):
        cols = slice(head * HD, (head + 1) * HD)
        value_cols = slice((heads + head) * HD, (heads + head + 1) * HD)
        q_cols = [slice((head * group + g) * HD, (head * group + g + 1) * HD) for g in range(group)]
        query = jnp.concatenate([query_ref[:, c] for c in q_cols], axis=0)
        grad = jnp.concatenate([grad_ref[:, c] for c in q_cols], axis=0)
        keys = jnp.concatenate([ref[:, cols] for ref in rim_pairs] + [key_ref[:, cols]], axis=0)
        values = jnp.concatenate(
            [ref[:, value_cols] for ref in rim_pairs] + [value_ref[:, cols]], axis=0
        )
        scores = jnp.where(keep, dot_f32(keys, query, NT) * scale, SCORE_FLOOR)
        weights = jnp.exp(scores - jnp.max(scores, axis=0, keepdims=True))
        probs = weights * (1.0 / jnp.sum(weights, axis=0, keepdims=True))
        probs_low = probs.astype(jnp.bfloat16)
        dprobs = dot_f32(values, grad, NT)
        delta = jnp.sum(probs_low.astype(jnp.float32) * dprobs, axis=0, keepdims=True)
        dscores = (probs * (dprobs - delta)).astype(jnp.bfloat16)
        query_part = (dot_f32(dscores, keys, TN) * scale).astype(jnp.bfloat16)
        for g, c in enumerate(q_cols):
            outs[0][:, c] = query_part[g * tok : (g + 1) * tok]
        key_part = dot_f32(dscores, query) * scale
        value_part = dot_f32(probs_low, grad)
        if hops == 1:
            first = place == 0
            key_rim, key_own = key_part[:tok], key_part[tok:]
            value_rim, value_own = value_part[:tok], value_part[tok:]
            outs[1][:, cols] = jnp.where(first, value_own, key_rim).astype(jnp.bfloat16)
            outs[2][:, cols] = jnp.where(first, key_own, value_rim).astype(jnp.bfloat16)
            outs[3][:, cols] = key_own.astype(jnp.bfloat16)
            outs[4][:, cols] = value_own.astype(jnp.bfloat16)
            outs[5][:, cols] = value_rim.astype(jnp.bfloat16)
        else:
            outs[1][:, cols] = key_part.astype(jnp.bfloat16)
            outs[2][:, cols] = value_part.astype(jnp.bfloat16)


def attend(chunk, place, segs, queries, out_grad, keys, values, rim_pairs, rim_segs, held):
    hops = len(rim_pairs)
    tok = queries.shape[0]
    group = queries.shape[1] // keys.shape[1]
    width = keys.shape[1] // CHUNKS
    span = (hops + 1) * tok
    whole = lambda *shape: pl.BlockSpec(shape, lambda i, *_: (0,) * len(shape))
    part = lambda *shape: pl.BlockSpec(shape, lambda i, *_: (0, chunk))
    seg_row = pl.BlockSpec((SEG_ROWS, tok), lambda i, *_: (tok // SEG_ROWS, 0))
    out_shapes = [(tok, group * width)]
    if hops == 1:
        out_shapes += [(tok, width)] * 5
        in_place = (0, 5)
    else:
        out_shapes += [(span, width)] * 2
        in_place = (0,)
    out_specs, out_types = [], []
    for place_of, (rows, columns) in enumerate(out_shapes):
        shared = place_of in in_place
        out_specs.append(part(rows, columns) if shared else whole(rows, columns))
        columns = columns * CHUNKS if shared else columns
        out_types.append(jax.ShapeDtypeStruct((rows, columns), jnp.bfloat16))
    operands = [place, segs, queries, out_grad, keys, values, *rim_pairs, *rim_segs]
    aliases = {len(operands) + n: in_place[n] for n in range(len(held))}
    return pl.pallas_call(
        partial(attention_kernel, hops, group, len(out_shapes)),
        grid_spec=pltpu.PrefetchScalarGridSpec(
            num_scalar_prefetch=1,
            grid=(1,),
            in_specs=[
                whole(1, tok),
                part(tok, group * width),
                part(tok, group * width),
                part(tok, width),
                part(tok, width),
            ]
            + [whole(tok, 2 * width)] * hops
            + [seg_row] * hops
            + [pl.BlockSpec(memory_space=pl.ANY)] * len(held),
            out_specs=out_specs,
        ),
        out_shape=out_types,
        input_output_aliases=aliases,
        compiler_params=pltpu.CompilerParams(vmem_limit_bytes=48 * MIB),
        cost_estimate=SMALL,
    )(*operands, *held)


def product_kernel(traces, *refs):
    own_ref, other_ref = refs[:2]
    grad_refs = refs[2 : 2 + traces]
    out_ref = refs[2 + traces]
    features = jnp.concatenate(
        [ref[t] for t in range(traces) for ref in (own_ref, other_ref)], axis=1
    )
    grads = jnp.concatenate([ref[...] for ref in grad_refs], axis=0)
    out_ref[...] = dot_f32(features, grads).astype(out_ref.dtype)


def product(features, grads, dtype):
    traces, rows, _ = features[0].shape
    width = grads[0].shape[1]
    return pl.pallas_call(
        partial(product_kernel, traces),
        out_shape=jax.ShapeDtypeStruct((rows, width), dtype),
        compiler_params=pltpu.CompilerParams(vmem_limit_bytes=48 * MIB),
        cost_estimate=SMALL,
    )(*features, *grads)


def finish_kernel(half_ref, last_ref, *refs):
    rows = last_ref.shape[0]
    refs[-1][...] = half_ref[rows:] + last_ref[...].astype(jnp.float32)


def finish(chunk, half, last, held):
    rows, width = last.shape
    return pl.pallas_call(
        finish_kernel,
        grid=(1,),
        in_specs=[
            pl.BlockSpec(half.shape, lambda i: (0, 0)),
            pl.BlockSpec(last.shape, lambda i: (0, 0)),
        ]
        + [pl.BlockSpec(memory_space=pl.ANY)] * len(held),
        out_specs=pl.BlockSpec((rows, width), lambda i: (0, chunk)),
        out_shape=jax.ShapeDtypeStruct((rows, width * CHUNKS), jnp.float32),
        input_output_aliases={2: 0} if held else {},
        cost_estimate=SMALL,
    )(half, last, *held)


def local(hidden_in, queries, key_states, value_states, out_grad, segment_ids):
    tok = queries.shape[1]
    key_width = key_states.shape[2]
    width = key_width // CHUNKS
    ctx_count = lax.axis_size("ctx")
    hops = min(WIN // tok, ctx_count - 1)
    place = lax.axis_index("ctx")
    first = place == 0
    place_arg = place.astype(jnp.int32).reshape(1)

    dp_count = lax.axis_size("dp")
    slow_count, core_count = 4, 2
    mid_count = dp_count // (slow_count * core_count)
    dp_place = lax.axis_index("dp")
    core_at = dp_place % core_count
    mid_at = dp_place // core_count % mid_count
    slow_at = dp_place // (core_count * mid_count)

    def dp_send(value, move):
        pairs = []
        for source in range(dp_count):
            core = source % core_count
            mid = source // core_count % mid_count
            slow = source // (core_count * mid_count)
            slow, mid, core = move(slow, mid, core)
            pairs.append((source, (slow * mid_count + mid) * core_count + core))
        return lax.ppermute(value, "dp", pairs)

    swap_core = lambda slow, mid, core: (slow, mid, core ^ 1)
    mid_by = lambda step: lambda slow, mid, core: (slow, (mid + step) % mid_count, core)
    flip_slow = lambda bit: lambda slow, mid, core: (slow ^ bit, mid, core)
    swap_ctx = [(c, c ^ 1) for c in range(ctx_count)]

    own_keys, own_values = key_states[0], value_states[0]

    steps = range(hops, 0, -1)
    seg_rows = jnp.broadcast_to(segment_ids.astype(jnp.bfloat16), (SEG_ROWS, tok))
    seg_rows = jnp.pad(seg_rows, ((0, 0), (0, 2 * width - tok)))
    rim_pairs = []
    for chunk in range(CHUNKS):
        cols = slice(chunk * width, (chunk + 1) * width)
        pair = jnp.concatenate([own_keys[:, cols], own_values[:, cols]], axis=1)
        if chunk == 0:
            pair = jnp.concatenate([pair, seg_rows], axis=0)
        rim_pairs.append([shifted(pair, "ctx", step) for step in steps])

    rows = hidden_in.shape[2] // dp_count
    by_feature = hidden_in[0].T.reshape(slow_count, mid_count, core_count, rows, tok)
    pieces = []
    for step in range(mid_count):
        for flip in range(core_count):
            share = lax.dynamic_slice(
                by_feature,
                (0, (mid_at + step) % mid_count, core_at ^ flip, 0, 0),
                (slow_count, 1, 1, rows, tok),
            )
            share = jnp.concatenate(
                [lax.dynamic_index_in_dim(share, slow_at ^ turn, 0) for turn in (3, 1, 2, 0)]
            ).reshape(slow_count * rows, tok)
            away = lambda slow, mid, core: (slow, (mid + step) % mid_count, core ^ flip)
            pieces.append(share if step == flip == 0 else dp_send(share, away))
    features = jnp.stack(pieces)

    half_rows = slow_count // 2 * rows
    attended, columns, held = [], [], []
    for chunk in range(CHUNKS):
        outs = attend(
            chunk,
            place_arg,
            segment_ids,
            queries[0],
            out_grad[0],
            own_keys,
            own_values,
            rim_pairs[chunk],
            rim_pairs[0],
            held,
        )
        attended.append(outs)
        held = [outs[0], outs[5]] if hops == 1 else [outs[0]]
        if ctx_count != 2:
            continue
        _, sent, addend, key_own, value_own, _ = outs
        arrived = lax.ppermute(sent, "ctx", swap_ctx)
        late_keys = lax.ppermute(key_own, "ctx", [(1, 0)])
        if chunk == 0:
            arrived, late_keys, rim_pairs[1:] = lax.optimization_barrier(
                (arrived, late_keys, rim_pairs[1:])
            )
            features, rim_pairs[1:] = lax.optimization_barrier((features, rim_pairs[1:]))
            halves = [features[:, :half_rows], features[:, half_rows:]]
            halves = [(own, lax.ppermute(own, "ctx", swap_ctx)) for own in halves]
        elif chunk == 1:
            arrived, late_keys, halves[0] = lax.optimization_barrier((arrived, late_keys, halves[0]))
        total = (addend.astype(jnp.float32) + arrived.astype(jnp.float32)).astype(jnp.bfloat16)
        columns.append(
            jnp.concatenate(
                [jnp.where(first, total, value_own), jnp.where(first, late_keys, total)], axis=0
            )
        )
    query_grad = held[0]

    if ctx_count == 2:
        key_grad = jnp.where(
            first,
            jnp.concatenate([block[:tok] for block in columns], axis=1),
            jnp.concatenate([outs[3] for outs in attended], axis=1),
        )
    else:
        key_rows = jnp.concatenate([outs[1] for outs in attended], axis=1)
        value_rows = jnp.concatenate([outs[2] for outs in attended], axis=1)
        totals = [part[hops * tok :].astype(jnp.float32) for part in (key_rows, value_rows)]
        for step in range(1, hops + 1):
            low = (hops - step) * tok
            totals = [
                total + shifted(part[low : low + tok], "ctx", -step).astype(jnp.float32)
                for total, part in zip(totals, (key_rows, value_rows))
            ]
        key_grad, value_grad = (total.astype(jnp.bfloat16) for total in totals)
        both = lax.all_to_all(
            jnp.concatenate([key_grad, value_grad], axis=1),
            "ctx",
            split_axis=1,
            concat_axis=0,
            tiled=True,
        )
        columns = jnp.split(both, CHUNKS, axis=1)
        every = lax.all_gather(features, "ctx", axis=2, tiled=True)
        halves = [
            tuple(jnp.split(every[:, low : low + half_rows], 2, axis=2)) for low in (0, half_rows)
        ]

    held = []
    for chunk, block in enumerate(columns):
        near = [block] + [dp_send(block, mid_by(step)) for step in range(1, mid_count)]
        grads = [piece for near_one in near for piece in (near_one, dp_send(near_one, swap_core))]
        sent = product(halves[0], grads, jnp.bfloat16)
        kept = product(halves[1], grads, jnp.float32)
        if chunk == 0 and ctx_count == 2:
            value_rim, sent = lax.optimization_barrier((attended[-1][5], sent))
            returned = lax.ppermute(value_rim, "ctx", [(1, 0)])
            value_own = jnp.concatenate([outs[4] for outs in attended], axis=1)
            value_grad = (value_own.astype(jnp.float32) + returned.astype(jnp.float32)).astype(
                jnp.bfloat16
            )
        half = kept + dp_send(sent, flip_slow(1)).astype(jnp.float32)
        last = dp_send(half[:rows].astype(jnp.bfloat16), flip_slow(2))
        held = [finish(chunk, half, last, held)]
    weight_grad = held[0]
    return (query_grad[None], key_grad[None], value_grad[None], weight_grad)


def solution(mesh):
    placed = (
        P("dp", "ctx", None),
        P("dp", "ctx", None),
        P("dp", "ctx", None),
        P("dp", "ctx", None),
        P("dp", "ctx", None),
        P("dp", "ctx"),
    )
    return jax.shard_map(
        local,
        mesh=mesh,
        in_specs=placed,
        out_specs=(
            P("dp", "ctx", None),
            P("dp", "ctx", None),
            P("dp", "ctx", None),
            P("dp", "ctx"),
        ),
        check_vma=False,
    )
```

```python
from functools import partial

import jax
import jax.numpy as jnp
from jax import lax
from jax.experimental import pallas as pl
from jax.experimental.pallas import tpu as pltpu
from jax.sharding import PartitionSpec as P

HD = 128
WIN = 1024
CHUNKS = 2
SPLIT = 2
SCORE_FLOOR = -1e30
MIB = 1024 * 1024
SEG_ROWS = 16
SMALL = pl.CostEstimate(flops=1024, bytes_accessed=1024, transcendentals=0)

NT = (((1,), (1,)), ((), ()))
TN = (((0,), (0,)), ((), ()))


def dot_f32(left, right, dims=(((1,), (0,)), ((), ()))):
    return lax.dot_general(left, right, dims, preferred_element_type=jnp.float32)


def shifted(value, axis, steps):
    count = lax.axis_size(axis)
    leading, last = (max(0, -steps), min(count, count - steps))
    return lax.ppermute(value, axis, [(source, source + steps) for source in range(leading, last)])


def attention_kernel(hops, group, outs_count, place_ref, *refs):
    segs_ref, query_ref, grad_ref, key_ref, value_ref = refs[:5]
    rim_refs = refs[5 : 5 + 2 * hops]
    rim_segs = rim_refs[hops:]
    rim_pairs = rim_refs[:hops]
    outs = refs[-outs_count:]
    tok = query_ref.shape[0]
    heads = key_ref.shape[1] // HD
    rim = hops * tok
    span = rim + tok
    place = place_ref[0]
    scale = HD**-0.5

    query_segs = segs_ref[...].astype(jnp.float32)
    key_cols = [
        jnp.transpose(jnp.broadcast_to(ref[...].astype(jnp.float32)[:1], (tok, tok)))
        for ref in (*rim_segs, segs_ref)
    ]
    key_segs = jnp.concatenate(key_cols, axis=0)
    key_at = lax.broadcasted_iota(jnp.int32, (span, tok), 0)
    distance = rim + lax.broadcasted_iota(jnp.int32, (span, tok), 1) - key_at
    allowed = (
        (key_at >= rim - place * tok)
        & (distance >= 0)
        & (distance < WIN)
        & (key_segs == query_segs)
    )
    floor = jnp.where(allowed, 0.0, SCORE_FLOOR)
    floor = jnp.concatenate([floor] * group, axis=1)
    keep = floor == 0.0

    for head in range(heads):
        cols = slice(head * HD, (head + 1) * HD)
        value_cols = slice((heads + head) * HD, (heads + head + 1) * HD)
        q_cols = [slice((head * group + g) * HD, (head * group + g + 1) * HD) for g in range(group)]
        query = jnp.concatenate([query_ref[:, c] for c in q_cols], axis=0)
        grad = jnp.concatenate([grad_ref[:, c] for c in q_cols], axis=0)
        keys = jnp.concatenate([ref[:, cols] for ref in rim_pairs] + [key_ref[:, cols]], axis=0)
        values = jnp.concatenate(
            [ref[:, value_cols] for ref in rim_pairs] + [value_ref[:, cols]], axis=0
        )
        scores = jnp.where(keep, dot_f32(keys, query, NT) * scale, SCORE_FLOOR)
        weights = jnp.exp(scores - jnp.max(scores, axis=0, keepdims=True))
        probs = weights * (1.0 / jnp.sum(weights, axis=0, keepdims=True))
        probs_low = probs.astype(jnp.bfloat16)
        dprobs = dot_f32(values, grad, NT)
        delta = jnp.sum(probs_low.astype(jnp.float32) * dprobs, axis=0, keepdims=True)
        dscores = (probs * (dprobs - delta)).astype(jnp.bfloat16)
        query_part = (dot_f32(dscores, keys, TN) * scale).astype(jnp.bfloat16)
        for g, c in enumerate(q_cols):
            outs[0][:, c] = query_part[g * tok : (g + 1) * tok]
        key_part = dot_f32(dscores, query) * scale
        value_part = dot_f32(probs_low, grad)
        if hops == 1:
            first = place == 0
            key_rim, key_own = key_part[:tok], key_part[tok:]
            value_rim, value_own = value_part[:tok], value_part[tok:]
            outs[1][:, cols] = jnp.where(first, value_own, key_rim).astype(jnp.bfloat16)
            outs[2][:, cols] = jnp.where(first, key_own, value_rim).astype(jnp.bfloat16)
            outs[3][:, cols] = key_own.astype(jnp.bfloat16)
            outs[4][:, cols] = value_own.astype(jnp.bfloat16)
            outs[5][:, cols] = value_rim.astype(jnp.bfloat16)
        else:
            outs[1][:, cols] = key_part.astype(jnp.bfloat16)
            outs[2][:, cols] = value_part.astype(jnp.bfloat16)


def attend(chunk, place, segs, queries, out_grad, keys, values, rim_pairs, rim_segs):
    hops = len(rim_pairs)
    tok = queries.shape[0]
    group = queries.shape[1] // keys.shape[1]
    width = keys.shape[1] // CHUNKS
    span = (hops + 1) * tok
    whole = lambda *shape: pl.BlockSpec(shape, lambda i, *_: (0,) * len(shape))
    part = lambda *shape: pl.BlockSpec(shape, lambda i, *_: (0, chunk))
    seg_row = pl.BlockSpec((SEG_ROWS, tok), lambda i, *_: (tok // SEG_ROWS, 0))
    out_shapes = [(tok, group * width)]
    out_shapes += [(tok, width)] * 5 if hops == 1 else [(span, width)] * 2
    operands = [place, segs, queries, out_grad, keys, values, *rim_pairs, *rim_segs]
    return pl.pallas_call(
        partial(attention_kernel, hops, group, len(out_shapes)),
        grid_spec=pltpu.PrefetchScalarGridSpec(
            num_scalar_prefetch=1,
            grid=(1,),
            in_specs=[
                whole(1, tok),
                part(tok, group * width),
                part(tok, group * width),
                part(tok, width),
                part(tok, width),
            ]
            + [whole(tok, 2 * width)] * hops
            + [seg_row] * hops,
            out_specs=[whole(*shape) for shape in out_shapes],
        ),
        out_shape=[jax.ShapeDtypeStruct(shape, jnp.bfloat16) for shape in out_shapes],
        compiler_params=pltpu.CompilerParams(vmem_limit_bytes=48 * MIB),
        cost_estimate=SMALL,
    )(*operands)


def product_kernel(traces, *refs):
    own_refs, first_ref, rest_ref = refs[:traces], refs[traces], refs[traces + 1]
    grad_refs = refs[traces + 2 : 2 * traces + 2]
    outs = refs[2 * traces + 2 :]
    away = [first_ref[...]] + [rest_ref[t] for t in range(traces - 1)]
    features = jnp.concatenate(
        [piece for t in range(traces) for piece in (own_refs[t][...], away[t])], axis=1
    )
    grads = jnp.concatenate([ref[...] for ref in grad_refs], axis=0)
    width = outs[0].shape[1]
    for n, out in enumerate(outs):
        out[...] = dot_f32(features, grads[:, n * width : (n + 1) * width]).astype(out.dtype)


def product(half, own, first_away, rest_away, grads, dtype):
    traces, (rows, tok) = len(own), own[0].shape
    rows //= 2
    width = grads[0].shape[1] // SPLIT
    half_of = lambda array: pl.BlockSpec((rows, array.shape[1]), lambda i: (half, 0))
    whole = lambda array: pl.BlockSpec(array.shape, lambda i: (0,) * array.ndim)
    return pl.pallas_call(
        partial(product_kernel, traces),
        grid=(1,),
        in_specs=[half_of(piece) for piece in (*own, first_away)]
        + [whole(piece) for piece in (rest_away, *grads)],
        out_specs=[pl.BlockSpec((rows, width), lambda i: (0, 0))] * SPLIT,
        out_shape=[jax.ShapeDtypeStruct((rows, width), dtype)] * SPLIT,
        compiler_params=pltpu.CompilerParams(vmem_limit_bytes=48 * MIB),
        cost_estimate=SMALL,
    )(*own, first_away, rest_away, *grads)


def local(hidden_in, queries, key_states, value_states, out_grad, segment_ids):
    tok = queries.shape[1]
    key_width = key_states.shape[2]
    width = key_width // CHUNKS
    ctx_count = lax.axis_size("ctx")
    hops = min(WIN // tok, ctx_count - 1)
    place = lax.axis_index("ctx")
    first = place == 0
    place_arg = place.astype(jnp.int32).reshape(1)

    dp_count = lax.axis_size("dp")
    slow_count, core_count = 4, 2
    mid_count = dp_count // (slow_count * core_count)
    dp_place = lax.axis_index("dp")
    core_at = dp_place % core_count
    mid_at = dp_place // core_count % mid_count
    slow_at = dp_place // (core_count * mid_count)

    def dp_send(value, move):
        pairs = []
        for source in range(dp_count):
            core = source % core_count
            mid = source // core_count % mid_count
            slow = source // (core_count * mid_count)
            slow, mid, core = move(slow, mid, core)
            pairs.append((source, (slow * mid_count + mid) * core_count + core))
        return lax.ppermute(value, "dp", pairs)

    swap_core = lambda slow, mid, core: (slow, mid, core ^ 1)
    mid_by = lambda step: lambda slow, mid, core: (slow, (mid + step) % mid_count, core)
    flip_slow = lambda bit: lambda slow, mid, core: (slow ^ bit, mid, core)
    swap_ctx = [(c, c ^ 1) for c in range(ctx_count)]

    own_keys, own_values = key_states[0], value_states[0]

    steps = range(hops, 0, -1)
    seg_rows = jnp.broadcast_to(segment_ids.astype(jnp.bfloat16), (SEG_ROWS, tok))
    seg_rows = jnp.pad(seg_rows, ((0, 0), (0, 2 * width - tok)))
    rim_pairs = []
    for chunk in range(CHUNKS):
        cols = slice(chunk * width, (chunk + 1) * width)
        pair = jnp.concatenate([own_keys[:, cols], own_values[:, cols]], axis=1)
        if chunk == 0:
            pair = jnp.concatenate([pair, seg_rows], axis=0)
        rim_pairs.append([shifted(pair, "ctx", step) for step in steps])

    rows = hidden_in.shape[2] // dp_count
    by_feature = hidden_in[0].T.reshape(slow_count, mid_count, core_count, rows, tok)
    pieces = []
    for step in range(mid_count):
        for flip in range(core_count):
            share = lax.dynamic_slice(
                by_feature,
                (0, (mid_at + step) % mid_count, core_at ^ flip, 0, 0),
                (slow_count, 1, 1, rows, tok),
            )
            share = jnp.concatenate(
                [lax.dynamic_index_in_dim(share, slow_at ^ turn, 0) for turn in (3, 1, 2, 0)]
            ).reshape(slow_count * rows, tok)
            away = lambda slow, mid, core: (slow, (mid + step) % mid_count, core ^ flip)
            pieces.append(share if step == flip == 0 else dp_send(share, away))

    half_rows = slow_count // 2 * rows
    low_high = [(0, half_rows), (half_rows, 2 * half_rows)]

    attended = []
    for chunk in range(CHUNKS):
        if chunk > 0:
            rim_pairs[chunk], _ = lax.optimization_barrier((rim_pairs[chunk], attended[-1][1]))
        attended.append(
            attend(
                chunk,
                place_arg,
                segment_ids,
                queries[0],
                out_grad[0],
                own_keys,
                own_values,
                rim_pairs[chunk],
                rim_pairs[0],
            )
        )
    query_grad = jnp.concatenate([outs[0] for outs in attended], axis=1)

    if ctx_count == 2:
        first_away = lax.ppermute(pieces[0], "ctx", swap_ctx)
        columns, rest_away = [], []
        for chunk, (_, sent, addend, key_own, value_own, _) in enumerate(attended):
            if chunk > 0:
                sent, key_own, _ = lax.optimization_barrier((sent, key_own, arrived))
            arrived = lax.ppermute(sent, "ctx", swap_ctx)
            late_keys = lax.ppermute(key_own, "ctx", [(1, 0)])
            if chunk == 0:
                arrived, late_keys, first_away, *_ = lax.optimization_barrier(
                    (arrived, late_keys, first_away, rim_pairs[1:])
                )
            total = (addend.astype(jnp.float32) + arrived.astype(jnp.float32)).astype(jnp.bfloat16)
            block = jnp.concatenate(
                [jnp.where(first, total, value_own), jnp.where(first, late_keys, total)], axis=0
            )
            if chunk == 0:
                for low, high in low_high:
                    rest = jnp.stack([piece[low:high] for piece in pieces[1:]])
                    rest, block = lax.optimization_barrier((rest, block))
                    rest_away.append(lax.ppermute(rest, "ctx", swap_ctx))
            columns.append(block)
        key_grad = jnp.where(
            first,
            jnp.concatenate([block[:tok] for block in columns], axis=1),
            jnp.concatenate([outs[3] for outs in attended], axis=1),
        )
    else:
        key_rows = jnp.concatenate([outs[1] for outs in attended], axis=1)
        value_rows = jnp.concatenate([outs[2] for outs in attended], axis=1)
        totals = [part[hops * tok :].astype(jnp.float32) for part in (key_rows, value_rows)]
        for step in range(1, hops + 1):
            low = (hops - step) * tok
            totals = [
                total + shifted(part[low : low + tok], "ctx", -step).astype(jnp.float32)
                for total, part in zip(totals, (key_rows, value_rows))
            ]
        key_grad, value_grad = (total.astype(jnp.bfloat16) for total in totals)
        both = lax.all_to_all(
            jnp.concatenate([key_grad, value_grad], axis=1),
            "ctx",
            split_axis=1,
            concat_axis=0,
            tiled=True,
        )
        columns = jnp.split(both, CHUNKS, axis=1)
        every = lax.all_gather(jnp.stack(pieces), "ctx", axis=2, tiled=True)
        near, away = jnp.split(every, 2, axis=2)
        pieces, first_away = list(near), away[0]
        rest_away = [away[1:, low:high] for low, high in low_high]

    gathered = []
    for block in columns:
        near = [block] + [dp_send(block, mid_by(step)) for step in range(1, mid_count)]
        gathered.append(
            [piece for near_one in near for piece in (near_one, dp_send(near_one, swap_core))]
        )
    gathered[-1], rest_away[1] = lax.optimization_barrier((gathered[-1], rest_away[1]))
    sent, kept = (
        [
            piece
            for grads in gathered
            for piece in product(half, pieces, first_away, rest_away[half], grads, dtype)
        ]
        for half, dtype in ((0, jnp.bfloat16), (1, jnp.float32))
    )
    if ctx_count == 2:
        value_rim = jnp.concatenate([outs[5] for outs in attended], axis=1)
        value_rim, sent[0] = lax.optimization_barrier((value_rim, sent[0]))
        returned = lax.ppermute(value_rim, "ctx", [(1, 0)])
        value_own = jnp.concatenate([outs[4] for outs in attended], axis=1)
        value_grad = (value_own.astype(jnp.float32) + returned.astype(jnp.float32)).astype(
            jnp.bfloat16
        )
    halves = [
        near + dp_send(far, flip_slow(1)).astype(jnp.float32) for near, far in zip(kept, sent)
    ]
    last = [dp_send(half[:rows].astype(jnp.bfloat16), flip_slow(2)) for half in halves]
    piece_width = halves[0].shape[1]
    weight_grad = jnp.zeros((rows, piece_width * len(halves)), jnp.float32)
    for n, (half, final) in enumerate(zip(halves, last)):
        weight_grad = lax.dynamic_update_slice(
            weight_grad, half[rows:] + final.astype(jnp.float32), (0, n * piece_width)
        )
    return (query_grad[None], key_grad[None], value_grad[None], weight_grad)


def solution(mesh):
    placed = (
        P("dp", "ctx", None),
        P("dp", "ctx", None),
        P("dp", "ctx", None),
        P("dp", "ctx", None),
        P("dp", "ctx", None),
        P("dp", "ctx"),
    )
    return jax.shard_map(
        local,
        mesh=mesh,
        in_specs=placed,
        out_specs=(
            P("dp", "ctx", None),
            P("dp", "ctx", None),
            P("dp", "ctx", None),
            P("dp", "ctx"),
        ),
        check_vma=False,
    )
```

```python
import math
from functools import partial

import jax
import jax.numpy as jnp
from jax import lax
from jax.experimental import pallas as pl
from jax.experimental.pallas import tpu as pltpu
from jax.sharding import PartitionSpec as P

HD = 128
WIN = 1024
CHUNKS = 2
SCORE_FLOOR = -1e30
MIB = 1024 * 1024
SEG_ROWS = 16
SMALL = pl.CostEstimate(flops=1024, bytes_accessed=1024, transcendentals=0)

NT = (((1,), (1,)), ((), ()))
TN = (((0,), (0,)), ((), ()))


def dot_f32(left, right, dims=(((1,), (0,)), ((), ()))):
    return lax.dot_general(left, right, dims, preferred_element_type=jnp.float32)


def shifted(value, axis, steps):
    count = lax.axis_size(axis)
    leading, last = (max(0, -steps), min(count, count - steps))
    return lax.ppermute(value, axis, [(source, source + steps) for source in range(leading, last)])


def attention_kernel(hops, group, outs_count, place_ref, *refs):
    segs_ref, query_ref, grad_ref, key_ref, value_ref = refs[:5]
    rim_refs = refs[5 : 5 + 2 * hops]
    rim_segs = rim_refs[hops:]
    rim_pairs = rim_refs[:hops]
    outs = refs[-outs_count:]
    tok = query_ref.shape[0]
    heads = key_ref.shape[1] // HD
    rim = hops * tok
    span = rim + tok
    place = place_ref[0]
    scale = HD**-0.5

    query_segs = segs_ref[...].astype(jnp.float32)
    key_cols = [
        jnp.transpose(jnp.broadcast_to(ref[...].astype(jnp.float32)[:1], (tok, tok)))
        for ref in (*rim_segs, segs_ref)
    ]
    key_segs = jnp.concatenate(key_cols, axis=0)
    key_at = lax.broadcasted_iota(jnp.int32, (span, tok), 0)
    distance = rim + lax.broadcasted_iota(jnp.int32, (span, tok), 1) - key_at
    allowed = (
        (key_at >= rim - place * tok)
        & (distance >= 0)
        & (distance < WIN)
        & (key_segs == query_segs)
    )
    floor = jnp.where(allowed, 0.0, SCORE_FLOOR)
    floor = jnp.concatenate([floor] * group, axis=1)
    keep = floor == 0.0

    for head in range(heads):
        cols = slice(head * HD, (head + 1) * HD)
        value_cols = slice((heads + head) * HD, (heads + head + 1) * HD)
        q_cols = [slice((head * group + g) * HD, (head * group + g + 1) * HD) for g in range(group)]
        query = jnp.concatenate([query_ref[:, c] for c in q_cols], axis=0)
        grad = jnp.concatenate([grad_ref[:, c] for c in q_cols], axis=0)
        keys = jnp.concatenate([ref[:, cols] for ref in rim_pairs] + [key_ref[:, cols]], axis=0)
        values = jnp.concatenate(
            [ref[:, value_cols] for ref in rim_pairs] + [value_ref[:, cols]], axis=0
        )
        scores = jnp.where(keep, dot_f32(keys, query, NT) * scale, SCORE_FLOOR)
        weights = jnp.exp(scores - jnp.max(scores, axis=0, keepdims=True))
        probs = weights * (1.0 / jnp.sum(weights, axis=0, keepdims=True))
        probs_low = probs.astype(jnp.bfloat16)
        dprobs = dot_f32(values, grad, NT)
        delta = jnp.sum(probs_low.astype(jnp.float32) * dprobs, axis=0, keepdims=True)
        dscores = (probs * (dprobs - delta)).astype(jnp.bfloat16)
        query_part = (dot_f32(dscores, keys, TN) * scale).astype(jnp.bfloat16)
        for g, c in enumerate(q_cols):
            outs[0][:, c] = query_part[g * tok : (g + 1) * tok]
        key_part = dot_f32(dscores, query) * scale
        value_part = dot_f32(probs_low, grad)
        if hops == 1:
            first = place == 0
            key_rim, key_own = key_part[:tok], key_part[tok:]
            value_rim, value_own = value_part[:tok], value_part[tok:]
            outs[1][:, cols] = jnp.where(first, value_own, key_rim).astype(jnp.bfloat16)
            outs[2][:, cols] = jnp.where(first, key_own, value_rim).astype(jnp.bfloat16)
            outs[3][:, cols] = key_own.astype(jnp.bfloat16)
            outs[4][:, cols] = value_own.astype(jnp.bfloat16)
            outs[5][:, cols] = value_rim.astype(jnp.bfloat16)
        else:
            outs[1][:, cols] = key_part.astype(jnp.bfloat16)
            outs[2][:, cols] = value_part.astype(jnp.bfloat16)


def attend(chunk, place, segs, queries, out_grad, keys, values, rim_pairs, rim_segs):
    hops = len(rim_pairs)
    tok = queries.shape[0]
    group = queries.shape[1] // keys.shape[1]
    width = keys.shape[1] // CHUNKS
    span = (hops + 1) * tok
    whole = lambda *shape: pl.BlockSpec(shape, lambda i, *_: (0,) * len(shape))
    part = lambda *shape: pl.BlockSpec(shape, lambda i, *_: (0, chunk))
    seg_row = pl.BlockSpec((SEG_ROWS, tok), lambda i, *_: (tok // SEG_ROWS, 0))
    out_shapes = [(tok, group * width)]
    out_shapes += [(tok, width)] * 5 if hops == 1 else [(span, width)] * 2
    operands = [place, segs, queries, out_grad, keys, values, *rim_pairs, *rim_segs]
    return pl.pallas_call(
        partial(attention_kernel, hops, group, len(out_shapes)),
        grid_spec=pltpu.PrefetchScalarGridSpec(
            num_scalar_prefetch=1,
            grid=(1,),
            in_specs=[
                whole(1, tok),
                part(tok, group * width),
                part(tok, group * width),
                part(tok, width),
                part(tok, width),
            ]
            + [whole(tok, 2 * width)] * hops
            + [seg_row] * hops,
            out_specs=[whole(*shape) for shape in out_shapes],
        ),
        out_shape=[jax.ShapeDtypeStruct(shape, jnp.bfloat16) for shape in out_shapes],
        compiler_params=pltpu.CompilerParams(vmem_limit_bytes=24 * MIB),
        cost_estimate=SMALL,
    )(*operands)


def product_kernel(*refs):
    grad_refs, (send_ref, keep_ref) = refs[4:-2], refs[-2:]
    grads = jnp.concatenate([ref[t] for ref in grad_refs for t in range(ref.shape[0])], axis=0)
    rows = send_ref.shape[1]
    for core in range(2):
        near, far = refs[2 * core : 2 * core + 2]
        features = jnp.concatenate(
            [ref[t ^ core] for t in range(near.shape[0]) for ref in (near, far)], axis=1
        )
        total = dot_f32(features, grads)
        send_ref[core] = total[:rows].astype(jnp.bfloat16)
        keep_ref[core] = total[rows:]


def product(mine, other, grads):
    rows = mine[0].shape[1] // 2
    width = grads[0].shape[2]
    shape = (2, rows, width)
    moved = sum(math.prod(array.shape) for array in (*mine, *other, *grads)) * 2
    return pl.pallas_call(
        product_kernel,
        out_shape=[
            jax.ShapeDtypeStruct(shape, jnp.bfloat16),
            jax.ShapeDtypeStruct(shape, jnp.float32),
        ],
        compiler_params=pltpu.CompilerParams(vmem_limit_bytes=8 * MIB + 4 * moved),
        cost_estimate=SMALL,
    )(*mine, *other, *grads)


def local(hidden_in, queries, key_states, value_states, out_grad, segment_ids):
    tok = queries.shape[1]
    key_width = key_states.shape[2]
    width = key_width // CHUNKS
    ctx_count = lax.axis_size("ctx")
    hops = min(WIN // tok, ctx_count - 1)
    place = lax.axis_index("ctx")
    first = place == 0
    place_arg = place.astype(jnp.int32).reshape(1)

    dp_count = lax.axis_size("dp")
    slow_count, core_count = 4, 2
    mid_count = dp_count // (slow_count * core_count)
    dp_place = lax.axis_index("dp")
    core_at = dp_place % core_count
    mid_at = dp_place // core_count % mid_count
    slow_at = dp_place // (core_count * mid_count)

    def dp_send(value, move):
        pairs = []
        for source in range(dp_count):
            core = source % core_count
            mid = source // core_count % mid_count
            slow = source // (core_count * mid_count)
            slow, mid, core = move(slow, mid, core)
            pairs.append((source, (slow * mid_count + mid) * core_count + core))
        return lax.ppermute(value, "dp", pairs)

    swap_core = lambda slow, mid, core: (slow, mid, core ^ 1)
    mid_by = lambda step: lambda slow, mid, core: (slow, (mid + step) % mid_count, core)
    flip_slow = lambda bit: lambda slow, mid, core: (slow ^ bit, mid, core)
    swap_ctx = [(c, c ^ 1) for c in range(ctx_count)]

    own_keys, own_values = key_states[0], value_states[0]

    steps = range(hops, 0, -1)
    seg_rows = jnp.broadcast_to(segment_ids.astype(jnp.bfloat16), (SEG_ROWS, tok))
    seg_rows = jnp.pad(seg_rows, ((0, 0), (0, 2 * width - tok)))
    pairs = []
    for chunk in range(CHUNKS):
        cols = slice(chunk * width, (chunk + 1) * width)
        pair = jnp.concatenate([own_keys[:, cols], own_values[:, cols]], axis=1)
        pairs.append(pair if chunk else jnp.concatenate([pair, seg_rows], axis=0))
    pairs, hidden = lax.optimization_barrier((pairs, hidden_in[0]))
    rim_pairs = [[shifted(pair, "ctx", step) for step in steps] for pair in pairs]

    rows = hidden_in.shape[2] // dp_count
    by_feature = hidden.T.reshape(slow_count, mid_count, core_count, rows, tok)

    def share_of(step, turn):
        blocks = [
            lax.dynamic_slice(
                by_feature,
                (slow_at ^ turn ^ further, (mid_at + step) % mid_count, 0, 0, 0),
                (1, 1, core_count, rows, tok),
            )
            for further in (2, 0)
        ]
        return jnp.concatenate(blocks, axis=3).reshape(core_count, 2 * rows, tok)

    shares = []
    for step in range(mid_count):
        for turn in (0, 1):
            away = lambda slow, mid, core: (slow ^ turn, (mid + step) % mid_count, core)
            share = share_of(step, turn)
            shares.append(dp_send(share, away) if step or turn else share)

    attended = []
    for chunk in range(CHUNKS):
        if chunk > 0:
            rim_pairs[chunk], _ = lax.optimization_barrier((rim_pairs[chunk], attended[-1][1]))
        attended.append(
            attend(
                chunk,
                place_arg,
                segment_ids,
                queries[0],
                out_grad[0],
                own_keys,
                own_values,
                rim_pairs[chunk],
                rim_pairs[0],
            )
        )
    query_grad = jnp.concatenate([outs[0] for outs in attended], axis=1)
    shares = jnp.stack(shares)
    of_core = lambda core: lax.dynamic_index_in_dim(shares, core, 1, False)
    near = jnp.stack([of_core(core_at), dp_send(of_core(1 - core_at), swap_core)], axis=1)
    near = near.reshape(-1, 2 * rows, tok)

    if ctx_count == 2:
        columns = []
        for chunk, (_, sent, addend, key_own, value_own, _) in enumerate(attended):
            if chunk > 0:
                sent, key_own, _ = lax.optimization_barrier((sent, key_own, arrived))
            arrived = lax.ppermute(sent, "ctx", swap_ctx)
            late_keys = lax.ppermute(key_own, "ctx", [(1, 0)])
            if chunk == 0:
                arrived, late_keys, _ = lax.optimization_barrier(
                    (arrived, late_keys, rim_pairs[1:])
                )
            total = (addend.astype(jnp.float32) + arrived.astype(jnp.float32)).astype(jnp.bfloat16)
            block = jnp.concatenate(
                [jnp.where(first, total, value_own), jnp.where(first, late_keys, total)], axis=0
            )
            if chunk == 0:
                sent_near, block = lax.optimization_barrier((near, block))
                far = lax.ppermute(sent_near, "ctx", swap_ctx)
            columns.append(block)
        key_grad = jnp.where(
            first,
            jnp.concatenate([block[:tok] for block in columns], axis=1),
            jnp.concatenate([outs[3] for outs in attended], axis=1),
        )
    else:
        key_rows = jnp.concatenate([outs[1] for outs in attended], axis=1)
        value_rows = jnp.concatenate([outs[2] for outs in attended], axis=1)
        totals = [part[hops * tok :].astype(jnp.float32) for part in (key_rows, value_rows)]
        for step in range(1, hops + 1):
            low = (hops - step) * tok
            totals = [
                total + shifted(part[low : low + tok], "ctx", -step).astype(jnp.float32)
                for total, part in zip(totals, (key_rows, value_rows))
            ]
        key_grad, value_grad = (total.astype(jnp.bfloat16) for total in totals)
        both = lax.all_to_all(
            jnp.concatenate([key_grad, value_grad], axis=1),
            "ctx",
            split_axis=1,
            concat_axis=0,
            tiled=True,
        )
        columns = jnp.split(both, CHUNKS, axis=1)
        every = lax.all_gather(near, "ctx", axis=2, tiled=True)
        near, far = jnp.split(every, 2, axis=2)

    mine = [near, far]
    other = [dp_send(piece, swap_core) for piece in mine]
    sent, kept = [], []
    for chunk, block in enumerate(columns):
        cols = block.shape[1] // core_count
        of_core = lambda core: lax.dynamic_slice_in_dim(block, core * cols, cols, 1)
        block = jnp.stack([of_core(core_at), dp_send(of_core(1 - core_at), swap_core)])
        steps = range(1, mid_count)
        turned = dp_send(block, flip_slow(1))
        moved = [dp_send(block, mid_by(step)) for step in steps]
        if chunk % 2 == 0:
            both = [dp_send(turned, mid_by(step)) for step in steps]
        else:
            both = [dp_send(piece, flip_slow(1)) for piece in moved]
        grads = [block, turned] + [piece for pair in zip(moved, both) for piece in pair]
        for parts, part in zip((sent, kept), product(mine, other, grads)):
            parts.append(part)

    if ctx_count == 2:
        value_rim = jnp.concatenate([outs[5] for outs in attended], axis=1)
        value_rim, sent[0] = lax.optimization_barrier((value_rim, sent[0]))
        returned = lax.ppermute(value_rim, "ctx", [(1, 0)])
        value_own = jnp.concatenate([outs[4] for outs in attended], axis=1)
        value_grad = (value_own.astype(jnp.float32) + returned.astype(jnp.float32)).astype(
            jnp.bfloat16
        )
    totals = [
        near + dp_send(far, flip_slow(2)).astype(jnp.float32) for near, far in zip(kept, sent)
    ]
    finals = [(total[0], dp_send(total[1], swap_core)) for total in totals]
    weight_grad = jnp.concatenate(
        [
            jnp.where(core_at == at, mine, theirs)
            for mine, theirs in finals
            for at in range(core_count)
        ],
        axis=1,
    )
    return (query_grad[None], key_grad[None], value_grad[None], weight_grad)


def solution(mesh):
    placed = (
        P("dp", "ctx", None),
        P("dp", "ctx", None),
        P("dp", "ctx", None),
        P("dp", "ctx", None),
        P("dp", "ctx", None),
        P("dp", "ctx"),
    )
    return jax.shard_map(
        local,
        mesh=mesh,
        in_specs=placed,
        out_specs=(
            P("dp", "ctx", None),
            P("dp", "ctx", None),
            P("dp", "ctx", None),
            P("dp", "ctx"),
        ),
        check_vma=False,
    )
```

```python
from functools import partial

import jax
import jax.numpy as jnp
from jax import lax
from jax.experimental import pallas as pl
from jax.experimental.pallas import tpu as pltpu
from jax.sharding import PartitionSpec as P

HD = 128
WIN = 1024
CHUNKS = 2
SPLIT = 2
SCORE_FLOOR = -1e30
MIB = 1024 * 1024
SEG_ROWS = 16
SMALL = pl.CostEstimate(flops=1024, bytes_accessed=1024, transcendentals=0)

NT = (((1,), (1,)), ((), ()))
TN = (((0,), (0,)), ((), ()))


def dot_f32(left, right, dims=(((1,), (0,)), ((), ()))):
    return lax.dot_general(left, right, dims, preferred_element_type=jnp.float32)


def shifted(value, axis, steps):
    count = lax.axis_size(axis)
    leading, last = (max(0, -steps), min(count, count - steps))
    return lax.ppermute(value, axis, [(source, source + steps) for source in range(leading, last)])


def attention_kernel(hops, group, outs_count, place_ref, *refs):
    segs_ref, query_ref, grad_ref, key_ref, value_ref = refs[:5]
    rim_refs = refs[5 : 5 + 2 * hops]
    rim_segs = rim_refs[hops:]
    rim_pairs = rim_refs[:hops]
    outs = refs[-outs_count:]
    tok = query_ref.shape[0]
    heads = key_ref.shape[1] // HD
    rim = hops * tok
    span = rim + tok
    place = place_ref[0]
    scale = HD**-0.5

    query_segs = segs_ref[...].astype(jnp.float32)
    key_cols = [
        jnp.transpose(jnp.broadcast_to(ref[...].astype(jnp.float32)[:1], (tok, tok)))
        for ref in (*rim_segs, segs_ref)
    ]
    key_segs = jnp.concatenate(key_cols, axis=0)
    key_at = lax.broadcasted_iota(jnp.int32, (span, tok), 0)
    distance = rim + lax.broadcasted_iota(jnp.int32, (span, tok), 1) - key_at
    allowed = (
        (key_at >= rim - place * tok)
        & (distance >= 0)
        & (distance < WIN)
        & (key_segs == query_segs)
    )
    floor = jnp.where(allowed, 0.0, SCORE_FLOOR)
    floor = jnp.concatenate([floor] * group, axis=1)
    keep = floor == 0.0

    for head in range(heads):
        cols = slice(head * HD, (head + 1) * HD)
        value_cols = slice((heads + head) * HD, (heads + head + 1) * HD)
        q_cols = [slice((head * group + g) * HD, (head * group + g + 1) * HD) for g in range(group)]
        query = jnp.concatenate([query_ref[:, c] for c in q_cols], axis=0)
        grad = jnp.concatenate([grad_ref[:, c] for c in q_cols], axis=0)
        keys = jnp.concatenate([ref[:, cols] for ref in rim_pairs] + [key_ref[:, cols]], axis=0)
        values = jnp.concatenate(
            [ref[:, value_cols] for ref in rim_pairs] + [value_ref[:, cols]], axis=0
        )
        scores = jnp.where(keep, dot_f32(keys, query, NT) * scale, SCORE_FLOOR)
        weights = jnp.exp(scores - jnp.max(scores, axis=0, keepdims=True))
        probs = weights * (1.0 / jnp.sum(weights, axis=0, keepdims=True))
        probs_low = probs.astype(jnp.bfloat16)
        dprobs = dot_f32(values, grad, NT)
        delta = jnp.sum(probs_low.astype(jnp.float32) * dprobs, axis=0, keepdims=True)
        dscores = (probs * (dprobs - delta)).astype(jnp.bfloat16)
        query_part = (dot_f32(dscores, keys, TN) * scale).astype(jnp.bfloat16)
        for g, c in enumerate(q_cols):
            outs[0][:, c] = query_part[g * tok : (g + 1) * tok]
        key_part = dot_f32(dscores, query) * scale
        value_part = dot_f32(probs_low, grad)
        if hops == 1:
            first = place == 0
            key_rim, key_own = key_part[:tok], key_part[tok:]
            value_rim, value_own = value_part[:tok], value_part[tok:]
            outs[1][:, cols] = jnp.where(first, value_own, key_rim).astype(jnp.bfloat16)
            outs[2][:, cols] = jnp.where(first, key_own, value_rim).astype(jnp.bfloat16)
            outs[3][:, cols] = key_own.astype(jnp.bfloat16)
            outs[4][:, cols] = value_own.astype(jnp.bfloat16)
            outs[5][:, cols] = value_rim.astype(jnp.bfloat16)
        else:
            outs[1][:, cols] = key_part.astype(jnp.bfloat16)
            outs[2][:, cols] = value_part.astype(jnp.bfloat16)


def attend(chunk, place, segs, queries, out_grad, keys, values, rim_pairs, rim_segs):
    hops = len(rim_pairs)
    tok = queries.shape[0]
    group = queries.shape[1] // keys.shape[1]
    width = keys.shape[1] // CHUNKS
    span = (hops + 1) * tok
    whole = lambda *shape: pl.BlockSpec(shape, lambda i, *_: (0,) * len(shape))
    part = lambda *shape: pl.BlockSpec(shape, lambda i, *_: (0, chunk))
    seg_row = pl.BlockSpec((SEG_ROWS, tok), lambda i, *_: (0, 2 * width // tok))
    out_shapes = [(tok, group * width)]
    out_shapes += [(tok, width)] * 5 if hops == 1 else [(span, width)] * 2
    operands = [place, segs, queries, out_grad, keys, values, *rim_pairs, *rim_segs]
    return pl.pallas_call(
        partial(attention_kernel, hops, group, len(out_shapes)),
        grid_spec=pltpu.PrefetchScalarGridSpec(
            num_scalar_prefetch=1,
            grid=(1,),
            in_specs=[
                whole(1, tok),
                part(tok, group * width),
                part(tok, group * width),
                part(tok, width),
                part(tok, width),
            ]
            + [pl.BlockSpec((tok, 2 * width), lambda i, *_: (0, 0))] * hops
            + [seg_row] * hops,
            out_specs=[whole(*shape) for shape in out_shapes],
        ),
        out_shape=[jax.ShapeDtypeStruct(shape, jnp.bfloat16) for shape in out_shapes],
        compiler_params=pltpu.CompilerParams(vmem_limit_bytes=24 * MIB),
        cost_estimate=SMALL,
    )(*operands)


def product_kernel(traces, place_ref, *refs):
    own_refs, grad_refs, rest = refs[:traces], refs[traces : 2 * traces], refs[2 * traces :]
    away_ref, rest = rest[0], rest[1:]
    away = [away_ref[t] for t in range(traces)]
    if len(rest) > SPLIT:
        first = place_ref[0] == 0
        away = [jnp.where(first, rest[t][...], away[t]) for t in range(traces)]
    features = jnp.concatenate(
        [piece for t in range(traces) for piece in (own_refs[t][...], away[t])], axis=1
    )
    grads = jnp.concatenate([ref[...] for ref in grad_refs], axis=0)
    outs = rest[-SPLIT:]
    width = outs[0].shape[1]
    for n, out in enumerate(outs):
        out[...] = dot_f32(features, grads[:, n * width : (n + 1) * width]).astype(out.dtype)


def product(half, place, own, away, first_away, grads, dtype):
    traces, (rows, tok) = len(own), own[0].shape
    rows //= 2
    width = grads[0].shape[1] // SPLIT
    half_of = lambda array: pl.BlockSpec((rows, array.shape[1]), lambda i, *_: (half, 0))
    whole = lambda array: pl.BlockSpec(array.shape, lambda i, *_: (0,) * array.ndim)
    return pl.pallas_call(
        partial(product_kernel, traces),
        grid_spec=pltpu.PrefetchScalarGridSpec(
            num_scalar_prefetch=1,
            grid=(1,),
            in_specs=[half_of(piece) for piece in own]
            + [whole(piece) for piece in (*grads, away)]
            + [half_of(piece) for piece in first_away],
            out_specs=[pl.BlockSpec((rows, width), lambda i, *_: (0, 0))] * SPLIT,
        ),
        out_shape=[jax.ShapeDtypeStruct((rows, width), dtype)] * SPLIT,
        compiler_params=pltpu.CompilerParams(vmem_limit_bytes=24 * MIB),
        cost_estimate=SMALL,
    )(place, *own, *grads, away, *first_away)


def local(hidden_in, queries, key_states, value_states, out_grad, segment_ids):
    tok = queries.shape[1]
    key_width = key_states.shape[2]
    width = key_width // CHUNKS
    ctx_count = lax.axis_size("ctx")
    hops = min(WIN // tok, ctx_count - 1)
    place = lax.axis_index("ctx")
    first = place == 0
    place_arg = place.astype(jnp.int32).reshape(1)

    dp_count = lax.axis_size("dp")
    slow_count, core_count = 4, 2
    mid_count = dp_count // (slow_count * core_count)
    dp_place = lax.axis_index("dp")
    core_at = dp_place % core_count
    mid_at = dp_place // core_count % mid_count
    slow_at = dp_place // (core_count * mid_count)

    def dp_send(value, move, only_first=False):
        pairs = []
        for source in range(dp_count):
            core = source % core_count
            mid = source // core_count % mid_count
            slow = source // (core_count * mid_count)
            slow, mid, core = move(slow, mid, core)
            pairs.append((source, (slow * mid_count + mid) * core_count + core))
        if only_first:
            pairs = [(source * ctx_count, target * ctx_count) for source, target in pairs]
            return lax.ppermute(value, ("dp", "ctx"), pairs)
        return lax.ppermute(value, "dp", pairs)

    swap_core = lambda slow, mid, core: (slow, mid, core ^ 1)
    mid_by = lambda step: lambda slow, mid, core: (slow, (mid + step) % mid_count, core)
    flip_slow = lambda bit: lambda slow, mid, core: (slow ^ bit, mid, core)
    swap_ctx = [(c, c ^ 1) for c in range(ctx_count)]

    own_keys, own_values = key_states[0], value_states[0]

    steps = range(hops, 0, -1)
    hidden = hidden_in[0]
    rim_pairs = []
    late_hidden = []
    for chunk in range(CHUNKS):
        cols = slice(chunk * width, (chunk + 1) * width)
        parts = [own_keys[:, cols], own_values[:, cols]]
        if chunk == 0:
            parts.append(jnp.broadcast_to(segment_ids.astype(jnp.bfloat16), (tok, tok)))
        pair = jnp.concatenate(parts, axis=1)
        if ctx_count == 2:
            low = sum(array.shape[1] for array in late_hidden)
            wide = hidden.shape[1] - low if chunk == CHUNKS - 1 else pair.shape[1]
            pair = jnp.pad(pair, ((0, 0), (0, wide - pair.shape[1])))
            pair = jnp.where(first, pair, hidden[:, low : low + wide])
            arrived = lax.ppermute(pair, "ctx", swap_ctx)
            late_hidden.append(arrived)
            rim_pairs.append([arrived])
        else:
            rim_pairs.append([shifted(pair, "ctx", step) for step in steps])

    rows = hidden_in.shape[2] // dp_count

    def by_feature(array):
        array = array.T.reshape(slow_count, mid_count, core_count, rows, tok)
        turns = [lax.dynamic_index_in_dim(array, slow_at ^ turn, 0, False) for turn in (3, 1, 2, 0)]
        return jnp.stack(turns)

    def spread(array, only_first):
        found = []
        for step in range(mid_count):
            for flip in range(core_count):
                share = lax.dynamic_slice(
                    array,
                    (0, (mid_at + step) % mid_count, core_at ^ flip, 0, 0),
                    (array.shape[0], 1, 1, rows, tok),
                ).reshape(-1, tok)
                away = lambda slow, mid, core: (slow, (mid + step) % mid_count, core ^ flip)
                if step or flip:
                    share = dp_send(share, away, only_first)
                found.append(share)
        return found

    pieces = spread(by_feature(hidden), False)

    half_rows = slow_count // 2 * rows
    low_high = [(0, half_rows), (half_rows, 2 * half_rows)]

    attended = []
    for chunk in range(CHUNKS):
        if chunk > 0:
            rim_pairs[chunk], _ = lax.optimization_barrier((rim_pairs[chunk], attended[-1][1]))
        attended.append(
            attend(
                chunk,
                place_arg,
                segment_ids,
                queries[0],
                out_grad[0],
                own_keys,
                own_values,
                rim_pairs[chunk],
                rim_pairs[0],
            )
        )
    query_grad = jnp.concatenate([outs[0] for outs in attended], axis=1)

    if ctx_count == 2:
        late_hidden, pieces, _ = lax.optimization_barrier((late_hidden, pieces, attended[0][1]))
        first_away = spread(by_feature(jnp.concatenate(late_hidden, axis=1)), True)
        columns = []
        half_stack = lambda low, high: jnp.stack([piece[low:high] for piece in pieces])
        for chunk, (_, sent, addend, key_own, value_own, _) in enumerate(attended):
            if chunk > 0:
                sent, key_own, _ = lax.optimization_barrier((sent, key_own, arrived))
            arrived = lax.ppermute(sent, "ctx", swap_ctx)
            late_keys = lax.ppermute(key_own, "ctx", [(1, 0)])
            if chunk == 0:
                arrived, late_keys, _ = lax.optimization_barrier(
                    (arrived, late_keys, rim_pairs[1:])
                )
                sent_away = lax.ppermute(half_stack(*low_high[0]), "ctx", [(0, 1)])
            elif chunk == 1:
                arrived, late_keys, sent_away, first_away = lax.optimization_barrier(
                    (arrived, late_keys, sent_away, first_away)
                )
            total = (addend.astype(jnp.float32) + arrived.astype(jnp.float32)).astype(jnp.bfloat16)
            block = jnp.concatenate(
                [jnp.where(first, total, value_own), jnp.where(first, late_keys, total)], axis=0
            )
            if chunk == 0:
                rest, block = lax.optimization_barrier((half_stack(*low_high[1]), block))
                kept_away = lax.ppermute(rest, "ctx", [(0, 1)])
            columns.append(block)
        key_grad = jnp.where(
            first,
            jnp.concatenate([block[:tok] for block in columns], axis=1),
            jnp.concatenate([outs[3] for outs in attended], axis=1),
        )
    else:
        key_rows = jnp.concatenate([outs[1] for outs in attended], axis=1)
        value_rows = jnp.concatenate([outs[2] for outs in attended], axis=1)
        totals = [part[hops * tok :].astype(jnp.float32) for part in (key_rows, value_rows)]
        for step in range(1, hops + 1):
            low = (hops - step) * tok
            totals = [
                total + shifted(part[low : low + tok], "ctx", -step).astype(jnp.float32)
                for total, part in zip(totals, (key_rows, value_rows))
            ]
        key_grad, value_grad = (total.astype(jnp.bfloat16) for total in totals)
        both = lax.all_to_all(
            jnp.concatenate([key_grad, value_grad], axis=1),
            "ctx",
            split_axis=1,
            concat_axis=0,
            tiled=True,
        )
        columns = jnp.split(both, CHUNKS, axis=1)
        every = lax.all_gather(jnp.stack(pieces), "ctx", axis=2, tiled=True)
        near, away = jnp.split(every, 2, axis=2)
        pieces, first_away = list(near), []
        sent_away, kept_away = (away[:, low:high] for low, high in low_high)

    gathered = []
    for block in columns:
        near = [block] + [dp_send(block, mid_by(step)) for step in range(1, mid_count)]
        gathered.append(
            [piece for near_one in near for piece in (near_one, dp_send(near_one, swap_core))]
        )
    gathered[-1], kept_away = lax.optimization_barrier((gathered[-1], kept_away))
    sent = [
        piece
        for grads in gathered
        for piece in product(0, place_arg, pieces, sent_away, first_away, grads, jnp.bfloat16)
    ]
    kept = [
        piece
        for grads in gathered
        for piece in product(1, place_arg, pieces, kept_away, first_away, grads, jnp.float32)
    ]
    if ctx_count == 2:
        value_rim = jnp.concatenate([outs[5] for outs in attended], axis=1)
        value_rim, sent[-1] = lax.optimization_barrier((value_rim, sent[-1]))
        returned = lax.ppermute(value_rim, "ctx", [(1, 0)])
        value_own = jnp.concatenate([outs[4] for outs in attended], axis=1)
        value_grad = (value_own.astype(jnp.float32) + returned.astype(jnp.float32)).astype(
            jnp.bfloat16
        )
    halves = [
        near + dp_send(far, flip_slow(1)).astype(jnp.float32) for near, far in zip(kept, sent)
    ]
    last = [dp_send(half[:rows].astype(jnp.bfloat16), flip_slow(2)) for half in halves]
    piece_width = halves[0].shape[1]
    weight_grad = jnp.zeros((rows, piece_width * len(halves)), jnp.float32)
    for n, (half, final) in enumerate(zip(halves, last)):
        weight_grad = lax.dynamic_update_slice(
            weight_grad, half[rows:] + final.astype(jnp.float32), (0, n * piece_width)
        )
    return (query_grad[None], key_grad[None], value_grad[None], weight_grad)


def solution(mesh):
    placed = (
        P("dp", "ctx", None),
        P("dp", "ctx", None),
        P("dp", "ctx", None),
        P("dp", "ctx", None),
        P("dp", "ctx", None),
        P("dp", "ctx"),
    )
    return jax.shard_map(
        local,
        mesh=mesh,
        in_specs=placed,
        out_specs=(
            P("dp", "ctx", None),
            P("dp", "ctx", None),
            P("dp", "ctx", None),
            P("dp", "ctx"),
        ),
        check_vma=False,
    )
```

```python
from functools import partial

import jax
import jax.numpy as jnp
from jax import lax
from jax.experimental import pallas as pl
from jax.experimental.pallas import tpu as pltpu
from jax.sharding import PartitionSpec as P

HD = 128
WIN = 1024
CHUNKS = 2
SCORE_FLOOR = -1e30
MIB = 1024 * 1024
SEG_ROWS = 16
SMALL = pl.CostEstimate(flops=1024, bytes_accessed=1024, transcendentals=0)

NT = (((1,), (1,)), ((), ()))
TN = (((0,), (0,)), ((), ()))


def dot_f32(left, right, dims=(((1,), (0,)), ((), ()))):
    return lax.dot_general(left, right, dims, preferred_element_type=jnp.float32)


def shifted(value, axis, steps):
    count = lax.axis_size(axis)
    leading, last = (max(0, -steps), min(count, count - steps))
    return lax.ppermute(value, axis, [(source, source + steps) for source in range(leading, last)])


def attention_kernel(chunk, hops, group, place_ref, *refs):
    segs_ref, query_ref, grad_ref, key_ref, value_ref = refs[:5]
    rim_pairs, rim_segs, refs = refs[5 : 5 + hops], refs[5 + hops : 5 + 2 * hops], refs[5 + 2 * hops :]
    tok = query_ref.shape[0]
    heads = key_ref.shape[1] // HD
    rim = hops * tok
    span = rim + tok
    place = place_ref[0]
    scale = HD**-0.5

    query_segs = segs_ref[...].astype(jnp.float32)
    key_cols = [
        jnp.transpose(jnp.broadcast_to(ref[...].astype(jnp.float32)[:1], (tok, tok)))
        for ref in (*rim_segs, segs_ref)
    ]
    key_segs = jnp.concatenate(key_cols, axis=0)
    key_at = lax.broadcasted_iota(jnp.int32, (span, tok), 0)
    distance = rim + lax.broadcasted_iota(jnp.int32, (span, tok), 1) - key_at
    allowed = (
        (key_at >= rim - place * tok)
        & (distance >= 0)
        & (distance < WIN)
        & (key_segs == query_segs)
    )
    floor = jnp.where(allowed, 0.0, SCORE_FLOOR)
    floor = jnp.concatenate([floor] * group, axis=1)
    keep = floor == 0.0

    for head in range(heads):
        cols = slice(head * HD, (head + 1) * HD)
        value_cols = slice((heads + head) * HD, (heads + head + 1) * HD)
        q_cols = [slice((head * group + g) * HD, (head * group + g + 1) * HD) for g in range(group)]
        query = jnp.concatenate([query_ref[:, c] for c in q_cols], axis=0)
        grad = jnp.concatenate([grad_ref[:, c] for c in q_cols], axis=0)
        keys = jnp.concatenate([ref[:tok, cols] for ref in rim_pairs] + [key_ref[:, cols]], axis=0)
        values = jnp.concatenate(
            [ref[:tok, value_cols] for ref in rim_pairs] + [value_ref[:, cols]], axis=0
        )
        scores = jnp.where(keep, dot_f32(keys, query, NT) * scale, SCORE_FLOOR)
        weights = jnp.exp(scores - jnp.max(scores, axis=0, keepdims=True))
        probs = weights * (1.0 / jnp.sum(weights, axis=0, keepdims=True))
        probs_low = probs.astype(jnp.bfloat16)
        dprobs = dot_f32(values, grad, NT)
        delta = jnp.sum(probs_low.astype(jnp.float32) * dprobs, axis=0, keepdims=True)
        dscores = (probs * (dprobs - delta)).astype(jnp.bfloat16)
        query_part = (dot_f32(dscores, keys, TN) * scale).astype(jnp.bfloat16)
        key_part = dot_f32(dscores, query) * scale
        value_part = dot_f32(probs_low, grad)
        if hops == 1:
            piece_ref, query_out, sent, addend, key_out, value_out, rim_out = refs
            first = place == 0
            key_rim, key_own = key_part[:tok], key_part[tok:]
            value_rim, value_own = value_part[:tok], value_part[tok:]
            sent[:tok, cols] = jnp.where(first, value_own, key_rim).astype(jnp.bfloat16)
            low = (chunk * heads + head) * tok
            high = min(low + tok, piece_ref.shape[0])
            late = key_own.astype(jnp.bfloat16)
            if low < high:
                part = piece_ref[low:high]
                if high - low < tok:
                    part = jnp.concatenate([part, late[: tok - (high - low)]], axis=0)
                late = jnp.where(first, part, late)
            sent[tok:, cols] = late
            addend[:, cols] = jnp.where(first, key_own, value_rim).astype(jnp.bfloat16)
            key_out[:, cols] = key_own.astype(jnp.bfloat16)
            value_out[:, cols] = value_own.astype(jnp.bfloat16)
            rim_out[:, cols] = value_rim.astype(jnp.bfloat16)
        else:
            query_out = refs[0]
            refs[1][:, cols] = key_part.astype(jnp.bfloat16)
            refs[2][:, cols] = value_part.astype(jnp.bfloat16)
        for g, c in enumerate(q_cols):
            query_out[:, c] = query_part[g * tok : (g + 1) * tok]


def attend(chunk, place, segs, queries, out_grad, keys, values, rim_pairs, rim_segs, piece):
    hops = len(rim_pairs)
    tok = queries.shape[0]
    group = queries.shape[1] // keys.shape[1]
    width = keys.shape[1] // CHUNKS
    span = (hops + 1) * tok
    whole = lambda *shape: pl.BlockSpec(shape, lambda i, *_: (0,) * len(shape))
    part = lambda *shape: pl.BlockSpec(shape, lambda i, *_: (0, chunk))
    seg_row = pl.BlockSpec((SEG_ROWS, tok), lambda i, *_: (tok // SEG_ROWS, 0))
    out_shapes = [(tok, group * width)]
    if hops == 1:
        out_shapes += [(2 * tok, width)] + [(tok, width)] * 4
    else:
        out_shapes += [(span, width)] * 2
    operands = [place, segs, queries, out_grad, keys, values, *rim_pairs, *rim_segs, *piece]
    return pl.pallas_call(
        partial(attention_kernel, chunk, hops, group),
        grid_spec=pltpu.PrefetchScalarGridSpec(
            num_scalar_prefetch=1,
            grid=(1,),
            in_specs=[
                whole(1, tok),
                part(tok, group * width),
                part(tok, group * width),
                part(tok, width),
                part(tok, width),
            ]
            + [whole(tok, 2 * width)] * hops
            + [seg_row] * hops
            + [whole(*array.shape) for array in piece],
            out_specs=[whole(*shape) for shape in out_shapes],
        ),
        out_shape=[jax.ShapeDtypeStruct(shape, jnp.bfloat16) for shape in out_shapes],
        compiler_params=pltpu.CompilerParams(vmem_limit_bytes=48 * MIB),
        cost_estimate=SMALL,
    )(*operands)


def product_kernel(own_ref, others_ref, own_away_ref, others_away_ref, *refs):
    grads = jnp.concatenate([ref[...] for ref in refs[:-1]], axis=0)
    others = range(others_ref.shape[0])
    near = [own_ref[...]] + [others_ref[t] for t in others]
    away = [own_away_ref[...]] + [others_away_ref[t] for t in others]
    features = jnp.concatenate([piece for pair in zip(near, away) for piece in pair], axis=1)
    refs[-1][...] = dot_f32(features, grads).astype(refs[-1].dtype)


def product(half, own, others, own_away, others_away, grads, dtype):
    traces, rows, tok = others.shape
    rows //= 2
    width = grads[0].shape[1]
    of_half = lambda array: pl.BlockSpec((rows, array.shape[1]), lambda i: (half, 0))
    whole = lambda array: pl.BlockSpec(array.shape, lambda i: (0,) * array.ndim)
    return pl.pallas_call(
        product_kernel,
        grid=(1,),
        in_specs=[
            of_half(own),
            pl.BlockSpec((traces, rows, tok), lambda i: (0, half, 0)),
            of_half(own_away),
            whole(others_away),
        ]
        + [whole(piece) for piece in grads],
        out_specs=pl.BlockSpec((rows, width), lambda i: (0, 0)),
        out_shape=jax.ShapeDtypeStruct((rows, width), dtype),
        compiler_params=pltpu.CompilerParams(vmem_limit_bytes=48 * MIB),
        cost_estimate=SMALL,
    )(own, others, own_away, others_away, *grads)


def local(hidden_in, queries, key_states, value_states, out_grad, segment_ids):
    tok = queries.shape[1]
    key_width = key_states.shape[2]
    width = key_width // CHUNKS
    ctx_count = lax.axis_size("ctx")
    hops = min(WIN // tok, ctx_count - 1)
    place = lax.axis_index("ctx")
    first = place == 0
    place_arg = place.astype(jnp.int32).reshape(1)

    dp_count = lax.axis_size("dp")
    slow_count, core_count = 4, 2
    mid_count = dp_count // (slow_count * core_count)
    dp_place = lax.axis_index("dp")
    core_at = dp_place % core_count
    mid_at = dp_place // core_count % mid_count
    slow_at = dp_place // (core_count * mid_count)

    def dp_send(value, move):
        pairs = []
        for source in range(dp_count):
            core = source % core_count
            mid = source // core_count % mid_count
            slow = source // (core_count * mid_count)
            slow, mid, core = move(slow, mid, core)
            pairs.append((source, (slow * mid_count + mid) * core_count + core))
        return lax.ppermute(value, "dp", pairs)

    swap_core = lambda slow, mid, core: (slow, mid, core ^ 1)
    mid_by = lambda step: lambda slow, mid, core: (slow, (mid + step) % mid_count, core)
    flip_slow = lambda bit: lambda slow, mid, core: (slow ^ bit, mid, core)
    swap_ctx = [(c, c ^ 1) for c in range(ctx_count)]

    own_keys, own_values = key_states[0], value_states[0]

    rows = hidden_in.shape[2] // dp_count
    by_feature = hidden_in[0].T.reshape(slow_count, mid_count, core_count, rows, tok)
    by_feature = jnp.stack(
        [lax.dynamic_index_in_dim(by_feature, slow_at ^ turn, 0, False) for turn in (3, 1, 2, 0)]
    )
    of_mid = lambda at: lax.dynamic_index_in_dim(by_feature, at % mid_count, 1, False)
    mids = [of_mid(mid_at)]
    mids += [dp_send(of_mid(mid_at + step), mid_by(step)) for step in range(1, mid_count)]
    share_of = lambda array, core: lax.dynamic_index_in_dim(array, core, -3, False).reshape(
        array.shape[:-4] + (slow_count * rows, tok)
    )
    own_piece = share_of(mids[0], core_at)

    steps = range(hops, 0, -1)
    seg_rows = jnp.broadcast_to(segment_ids.astype(jnp.bfloat16), (SEG_ROWS, tok))
    seg_rows = jnp.pad(seg_rows, ((0, 0), (0, 2 * width - tok)))
    to_rows = lambda array: array.reshape(tok, -1, HD).transpose(1, 0, 2).reshape(-1, HD)
    rim_pairs = []
    for chunk in range(CHUNKS):
        cols = slice(chunk * width, (chunk + 1) * width)
        pair = jnp.concatenate([own_keys[:, cols], own_values[:, cols]], axis=1)
        if chunk == 0:
            pair = jnp.concatenate([pair, seg_rows], axis=0)
        if ctx_count == 2 and chunk == CHUNKS - 1:
            back = jnp.pad(own_piece, ((0, 2 * width - own_piece.shape[0]), (0, 0)))
            back = back.reshape(-1, tok, HD).transpose(1, 0, 2).reshape(tok, -1)
            rim_pairs.append([lax.ppermute(jnp.where(first, pair, back), "ctx", swap_ctx)])
        else:
            rim_pairs.append([shifted(pair, "ctx", step) for step in steps])

    half_rows = slow_count // 2 * rows
    low_high = [(0, half_rows), (half_rows, 2 * half_rows)]

    attended = []
    for chunk in range(CHUNKS):
        if chunk > 0:
            rim_pairs[chunk], _ = lax.optimization_barrier((rim_pairs[chunk], attended[-1][1]))
        attended.append(
            attend(
                chunk,
                place_arg,
                segment_ids,
                queries[0],
                out_grad[0],
                own_keys,
                own_values,
                rim_pairs[chunk],
                rim_pairs[0],
                [own_piece] if hops == 1 else [],
            )
        )
    query_grad = jnp.concatenate([outs[0] for outs in attended], axis=1)

    mids = jnp.stack(mids)
    kept_core, sent_core = share_of(mids, core_at), share_of(mids, 1 - core_at)
    other_core = dp_send(sent_core, swap_core)
    others = jnp.concatenate([kept_core[1:], other_core])

    if ctx_count == 2:
        columns, held_back, others_away = [], [], []
        for chunk, (_, sent, addend, key_own, value_own, _) in enumerate(attended):
            arrived = lax.ppermute(sent, "ctx", swap_ctx)
            held_back.append(to_rows(arrived[tok:]))
            if chunk == 0:
                arrived, _ = lax.optimization_barrier((arrived, rim_pairs[1:]))
            else:
                arrived, _ = lax.optimization_barrier((arrived, columns[-1]))
            total = (addend.astype(jnp.float32) + arrived[:tok].astype(jnp.float32)).astype(
                jnp.bfloat16
            )
            block = jnp.concatenate(
                [jnp.where(first, total, value_own), jnp.where(first, arrived[tok:], total)], axis=0
            )
            if chunk == 0:
                for low, high in low_high:
                    rest, block = lax.optimization_barrier((others[:, low:high], block))
                    others_away.append(lax.ppermute(rest, "ctx", swap_ctx))
            columns.append(block)
        piece_rows = own_piece.shape[0]
        own_away = jnp.where(
            first, to_rows(rim_pairs[-1][0])[:piece_rows], jnp.concatenate(held_back)[:piece_rows]
        )
        key_grad = jnp.where(
            first,
            jnp.concatenate([block[:tok] for block in columns], axis=1),
            jnp.concatenate([outs[3] for outs in attended], axis=1),
        )
    else:
        key_rows = jnp.concatenate([outs[1] for outs in attended], axis=1)
        value_rows = jnp.concatenate([outs[2] for outs in attended], axis=1)
        totals = [part[hops * tok :].astype(jnp.float32) for part in (key_rows, value_rows)]
        for step in range(1, hops + 1):
            low = (hops - step) * tok
            totals = [
                total + shifted(part[low : low + tok], "ctx", -step).astype(jnp.float32)
                for total, part in zip(totals, (key_rows, value_rows))
            ]
        key_grad, value_grad = (total.astype(jnp.bfloat16) for total in totals)
        both = lax.all_to_all(
            jnp.concatenate([key_grad, value_grad], axis=1),
            "ctx",
            split_axis=1,
            concat_axis=0,
            tiled=True,
        )
        columns = jnp.split(both, CHUNKS, axis=1)
        every = jnp.concatenate([own_piece[None], others])
        near, away = jnp.split(lax.all_gather(every, "ctx", axis=2, tiled=True), 2, axis=2)
        own_piece, others, own_away = near[0], near[1:], away[0]
        others_away = [away[1:, low:high] for low, high in low_high]

    gathered = []
    for block in columns:
        near = [block] + [dp_send(block, mid_by(step)) for step in range(1, mid_count)]
        gathered.append(near + [dp_send(near_one, swap_core) for near_one in near])
    together = lambda half, dtype: [
        product(half, own_piece, others, own_away, others_away[half], grads, dtype)
        for grads in gathered
    ]
    sent = together(0, jnp.bfloat16)
    others_away[1], _ = lax.optimization_barrier((others_away[1], sent))
    kept = together(1, jnp.float32)
    halves = [
        near + dp_send(far, flip_slow(1)).astype(jnp.float32) for near, far in zip(kept, sent)
    ]
    if ctx_count == 2:
        value_rim = jnp.concatenate([outs[5] for outs in attended], axis=1)
        value_rim, _ = lax.optimization_barrier((value_rim, halves[0]))
        returned = lax.ppermute(value_rim, "ctx", [(1, 0)])
        value_own = jnp.concatenate([outs[4] for outs in attended], axis=1)
        value_grad = (value_own.astype(jnp.float32) + returned.astype(jnp.float32)).astype(
            jnp.bfloat16
        )
    last = [dp_send(half[:rows].astype(jnp.bfloat16), flip_slow(2)) for half in halves]
    piece_width = halves[0].shape[1]
    weight_grad = jnp.zeros((rows, piece_width * len(halves)), jnp.float32)
    for n, (half, final) in enumerate(zip(halves, last)):
        weight_grad = lax.dynamic_update_slice(
            weight_grad, half[rows:] + final.astype(jnp.float32), (0, n * piece_width)
        )
    return (query_grad[None], key_grad[None], value_grad[None], weight_grad)


def solution(mesh):
    placed = (
        P("dp", "ctx", None),
        P("dp", "ctx", None),
        P("dp", "ctx", None),
        P("dp", "ctx", None),
        P("dp", "ctx", None),
        P("dp", "ctx"),
    )
    return jax.shard_map(
        local,
        mesh=mesh,
        in_specs=placed,
        out_specs=(
            P("dp", "ctx", None),
            P("dp", "ctx", None),
            P("dp", "ctx", None),
            P("dp", "ctx"),
        ),
        check_vma=False,
    )
```

```python
from functools import partial

import jax
import jax.numpy as jnp
from jax import lax
from jax.experimental import pallas as pl
from jax.experimental.pallas import tpu as pltpu
from jax.sharding import PartitionSpec as P

HD = 128
WIN = 1024
CHUNKS = 2
SCORE_FLOOR = -1e30
MIB = 1024 * 1024
SEG_ROWS = 16
SMALL = pl.CostEstimate(flops=1024, bytes_accessed=1024, transcendentals=0)

NT = (((1,), (1,)), ((), ()))
TN = (((0,), (0,)), ((), ()))


def dot_f32(left, right, dims=(((1,), (0,)), ((), ()))):
    return lax.dot_general(left, right, dims, preferred_element_type=jnp.float32)


def shifted(value, axis, steps):
    count = lax.axis_size(axis)
    leading, last = (max(0, -steps), min(count, count - steps))
    return lax.ppermute(value, axis, [(source, source + steps) for source in range(leading, last)])


def attention_kernel(chunk, hops, group, place_ref, *refs):
    segs_ref, query_ref, grad_ref, key_ref, value_ref = refs[:5]
    rim_pairs, rim_segs, refs = refs[5 : 5 + hops], refs[5 + hops : 5 + 2 * hops], refs[5 + 2 * hops :]
    tok = query_ref.shape[0]
    heads = key_ref.shape[1] // HD
    rim = hops * tok
    span = rim + tok
    place = place_ref[0]
    scale = HD**-0.5

    query_segs = segs_ref[:1].astype(jnp.float32)
    key_cols = [
        jnp.transpose(jnp.broadcast_to(ref[...].astype(jnp.float32)[:1], (tok, tok)))
        for ref in (*rim_segs, segs_ref)
    ]
    key_segs = jnp.concatenate(key_cols, axis=0)
    key_at = lax.broadcasted_iota(jnp.int32, (span, tok), 0)
    distance = rim + lax.broadcasted_iota(jnp.int32, (span, tok), 1) - key_at
    allowed = (
        (key_at >= rim - place * tok)
        & (distance >= 0)
        & (distance < WIN)
        & (key_segs == query_segs)
    )
    floor = jnp.where(allowed, 0.0, SCORE_FLOOR)
    floor = jnp.concatenate([floor] * group, axis=1)
    keep = floor == 0.0

    for head in range(heads):
        cols = slice(head * HD, (head + 1) * HD)
        value_cols = slice((heads + head) * HD, (heads + head + 1) * HD)
        q_cols = [slice((head * group + g) * HD, (head * group + g + 1) * HD) for g in range(group)]
        query = jnp.concatenate([query_ref[:, c] for c in q_cols], axis=0)
        grad = jnp.concatenate([grad_ref[:, c] for c in q_cols], axis=0)
        keys = jnp.concatenate([ref[:tok, cols] for ref in rim_pairs] + [key_ref[:, cols]], axis=0)
        values = jnp.concatenate(
            [ref[:tok, value_cols] for ref in rim_pairs] + [value_ref[:, cols]], axis=0
        )
        scores = jnp.where(keep, dot_f32(keys, query, NT) * scale, SCORE_FLOOR)
        weights = jnp.exp(scores - jnp.max(scores, axis=0, keepdims=True))
        probs = weights * (1.0 / jnp.sum(weights, axis=0, keepdims=True))
        probs_low = probs.astype(jnp.bfloat16)
        dprobs = dot_f32(values, grad, NT)
        delta = jnp.sum(probs_low.astype(jnp.float32) * dprobs, axis=0, keepdims=True)
        dscores = (probs * (dprobs - delta)).astype(jnp.bfloat16)
        query_part = (dot_f32(dscores, keys, TN) * scale).astype(jnp.bfloat16)
        key_part = dot_f32(dscores, query) * scale
        value_part = dot_f32(probs_low, grad)
        if hops == 1:
            piece_ref, query_out, sent, addend, key_out, value_out, rim_out = refs
            first = place == 0
            key_rim, key_own = key_part[:tok], key_part[tok:]
            value_rim, value_own = value_part[:tok], value_part[tok:]
            sent[:tok, cols] = jnp.where(first, value_own, key_rim).astype(jnp.bfloat16)
            low = (chunk * heads + head) * tok
            high = min(low + tok, piece_ref.shape[0])
            late = key_own.astype(jnp.bfloat16)
            if low < high:
                part = piece_ref[low:high]
                if high - low < tok:
                    part = jnp.concatenate([part, late[: tok - (high - low)]], axis=0)
                late = jnp.where(first, part, late)
            sent[tok:, cols] = late
            addend[:, cols] = jnp.where(first, key_own, value_rim).astype(jnp.bfloat16)
            key_out[:, cols] = key_own.astype(jnp.bfloat16)
            value_out[:, cols] = value_own.astype(jnp.bfloat16)
            rim_out[:, cols] = value_rim.astype(jnp.bfloat16)
        else:
            query_out = refs[0]
            refs[1][:, cols] = key_part.astype(jnp.bfloat16)
            refs[2][:, cols] = value_part.astype(jnp.bfloat16)
        for g, c in enumerate(q_cols):
            query_out[:, c] = query_part[g * tok : (g + 1) * tok]


def attend(chunk, place, segs, queries, out_grad, keys, values, rim_pairs, rim_segs, piece):
    hops = len(rim_pairs)
    tok = queries.shape[0]
    group = queries.shape[1] // keys.shape[1]
    width = keys.shape[1] // CHUNKS
    span = (hops + 1) * tok
    whole = lambda *shape: pl.BlockSpec(shape, lambda i, *_: (0,) * len(shape))
    part = lambda *shape: pl.BlockSpec(shape, lambda i, *_: (0, chunk))
    seg_row = pl.BlockSpec((SEG_ROWS, tok), lambda i, *_: (tok // SEG_ROWS, 0))
    out_shapes = [(tok, group * width)]
    if hops == 1:
        out_shapes += [(2 * tok, width)] + [(tok, width)] * 4
    else:
        out_shapes += [(span, width)] * 2
    operands = [place, segs, queries, out_grad, keys, values, *rim_pairs, *rim_segs, *piece]
    return pl.pallas_call(
        partial(attention_kernel, chunk, hops, group),
        grid_spec=pltpu.PrefetchScalarGridSpec(
            num_scalar_prefetch=1,
            grid=(1,),
            in_specs=[
                whole(SEG_ROWS, tok),
                part(tok, group * width),
                part(tok, group * width),
                part(tok, width),
                part(tok, width),
            ]
            + [whole(tok, 2 * width)] * hops
            + [seg_row] * hops
            + [whole(*array.shape) for array in piece],
            out_specs=[whole(*shape) for shape in out_shapes],
        ),
        out_shape=[jax.ShapeDtypeStruct(shape, jnp.bfloat16) for shape in out_shapes],
        compiler_params=pltpu.CompilerParams(vmem_limit_bytes=48 * MIB),
        cost_estimate=SMALL,
    )(*operands)


def product_kernel(own_ref, others_ref, own_away_ref, others_away_ref, *refs):
    grads = jnp.concatenate([ref[...] for ref in refs[:-1]], axis=0)
    others = range(others_ref.shape[0])
    near = [own_ref[...]] + [others_ref[t] for t in others]
    away = [own_away_ref[...]] + [others_away_ref[t] for t in others]
    features = jnp.concatenate([piece for pair in zip(near, away) for piece in pair], axis=1)
    refs[-1][...] = dot_f32(features, grads).astype(refs[-1].dtype)


def product(half, own, others, own_away, others_away, grads, dtype):
    traces, rows, tok = others.shape
    rows //= 2
    width = grads[0].shape[1]
    of_half = lambda array: pl.BlockSpec((rows, array.shape[1]), lambda i: (half, 0))
    whole = lambda array: pl.BlockSpec(array.shape, lambda i: (0,) * array.ndim)
    return pl.pallas_call(
        product_kernel,
        grid=(1,),
        in_specs=[
            of_half(own),
            pl.BlockSpec((traces, rows, tok), lambda i: (0, half, 0)),
            of_half(own_away),
            whole(others_away),
        ]
        + [whole(piece) for piece in grads],
        out_specs=pl.BlockSpec((rows, width), lambda i: (0, 0)),
        out_shape=jax.ShapeDtypeStruct((rows, width), dtype),
        compiler_params=pltpu.CompilerParams(vmem_limit_bytes=48 * MIB),
        cost_estimate=SMALL,
    )(own, others, own_away, others_away, *grads)


def local(hidden_in, queries, key_states, value_states, out_grad, segment_ids):
    tok = queries.shape[1]
    key_width = key_states.shape[2]
    width = key_width // CHUNKS
    ctx_count = lax.axis_size("ctx")
    hops = min(WIN // tok, ctx_count - 1)
    place = lax.axis_index("ctx")
    first = place == 0
    place_arg = place.astype(jnp.int32).reshape(1)

    dp_count = lax.axis_size("dp")
    slow_count, core_count = 4, 2
    mid_count = dp_count // (slow_count * core_count)
    dp_place = lax.axis_index("dp")
    core_at = dp_place % core_count
    mid_at = dp_place // core_count % mid_count
    slow_at = dp_place // (core_count * mid_count)

    def dp_send(value, move):
        pairs = []
        for source in range(dp_count):
            core = source % core_count
            mid = source // core_count % mid_count
            slow = source // (core_count * mid_count)
            slow, mid, core = move(slow, mid, core)
            pairs.append((source, (slow * mid_count + mid) * core_count + core))
        return lax.ppermute(value, "dp", pairs)

    swap_core = lambda slow, mid, core: (slow, mid, core ^ 1)
    mid_by = lambda step: lambda slow, mid, core: (slow, (mid + step) % mid_count, core)
    flip_slow = lambda bit: lambda slow, mid, core: (slow ^ bit, mid, core)
    swap_ctx = [(c, c ^ 1) for c in range(ctx_count)]

    own_keys, own_values = key_states[0], value_states[0]

    rows = hidden_in.shape[2] // dp_count
    by_feature = hidden_in[0].T.reshape(slow_count, mid_count, core_count, rows, tok)
    by_feature = jnp.stack(
        [lax.dynamic_index_in_dim(by_feature, slow_at ^ turn, 0, False) for turn in (3, 1, 2, 0)]
    )
    of_mid = lambda at: lax.dynamic_index_in_dim(by_feature, at % mid_count, 1, False)
    mids = [of_mid(mid_at)]
    mids += [dp_send(of_mid(mid_at + step), mid_by(step)) for step in range(1, mid_count)]
    share_of = lambda array, core: lax.dynamic_index_in_dim(array, core, -3, False).reshape(
        array.shape[:-4] + (slow_count * rows, tok)
    )
    own_piece = share_of(mids[0], core_at)

    steps = range(hops, 0, -1)
    seg_rows = jnp.broadcast_to(segment_ids.astype(jnp.bfloat16), (SEG_ROWS, tok))
    wide_rows = jnp.pad(seg_rows, ((0, 0), (0, 2 * width - tok)))
    to_rows = lambda array: array.reshape(tok, -1, HD).transpose(1, 0, 2).reshape(-1, HD)
    rim_pairs = []
    for chunk in range(CHUNKS):
        cols = slice(chunk * width, (chunk + 1) * width)
        pair = jnp.concatenate([own_keys[:, cols], own_values[:, cols]], axis=1)
        if chunk == 0:
            pair = jnp.concatenate([pair, wide_rows], axis=0)
        if ctx_count == 2 and chunk == CHUNKS - 1:
            back = jnp.pad(own_piece, ((0, 2 * width - own_piece.shape[0]), (0, 0)))
            back = back.reshape(-1, tok, HD).transpose(1, 0, 2).reshape(tok, -1)
            rim_pairs.append([lax.ppermute(jnp.where(first, pair, back), "ctx", swap_ctx)])
        else:
            rim_pairs.append([shifted(pair, "ctx", step) for step in steps])

    half_rows = slow_count // 2 * rows
    low_high = [(0, half_rows), (half_rows, 2 * half_rows)]

    mids = jnp.stack(mids)
    sent_core = share_of(mids, 1 - core_at)
    attended = []
    for chunk in range(CHUNKS):
        if chunk == 1:
            rim_pairs[1], sent_core, _ = lax.optimization_barrier(
                (rim_pairs[1], sent_core, attended[0][1])
            )
        attended.append(
            attend(
                chunk,
                place_arg,
                seg_rows,
                queries[0],
                out_grad[0],
                own_keys,
                own_values,
                rim_pairs[chunk],
                rim_pairs[0],
                [own_piece] if hops == 1 else [],
            )
        )
    kept_core = share_of(mids, core_at)
    other_core = dp_send(sent_core, swap_core)
    others = jnp.concatenate([kept_core[1:], other_core])

    if ctx_count == 2:
        columns, held_back, others_away = [], [], []
        for chunk, (_, sent, addend, key_own, value_own, _) in enumerate(attended):
            arrived = lax.ppermute(sent, "ctx", swap_ctx)
            held_back.append(to_rows(arrived[tok:]))
            if chunk == 0:
                arrived, _ = lax.optimization_barrier((arrived, rim_pairs[1:]))
            else:
                arrived, _ = lax.optimization_barrier((arrived, columns[-1]))
            total = (addend.astype(jnp.float32) + arrived[:tok].astype(jnp.float32)).astype(
                jnp.bfloat16
            )
            block = jnp.concatenate(
                [jnp.where(first, total, value_own), jnp.where(first, arrived[tok:], total)], axis=0
            )
            if chunk == 0:
                for low, high in low_high:
                    rest, block = lax.optimization_barrier((others[:, low:high], block))
                    others_away.append(lax.ppermute(rest, "ctx", swap_ctx))
            columns.append(block)
        piece_rows = own_piece.shape[0]
        own_away = jnp.where(
            first, to_rows(rim_pairs[-1][0])[:piece_rows], jnp.concatenate(held_back)[:piece_rows]
        )
        key_grad = jnp.where(
            first,
            jnp.concatenate([block[:tok] for block in columns], axis=1),
            jnp.concatenate([outs[3] for outs in attended], axis=1),
        )
    else:
        key_rows = jnp.concatenate([outs[1] for outs in attended], axis=1)
        value_rows = jnp.concatenate([outs[2] for outs in attended], axis=1)
        totals = [part[hops * tok :].astype(jnp.float32) for part in (key_rows, value_rows)]
        for step in range(1, hops + 1):
            low = (hops - step) * tok
            totals = [
                total + shifted(part[low : low + tok], "ctx", -step).astype(jnp.float32)
                for total, part in zip(totals, (key_rows, value_rows))
            ]
        key_grad, value_grad = (total.astype(jnp.bfloat16) for total in totals)
        both = lax.all_to_all(
            jnp.concatenate([key_grad, value_grad], axis=1),
            "ctx",
            split_axis=1,
            concat_axis=0,
            tiled=True,
        )
        columns = jnp.split(both, CHUNKS, axis=1)
        every = jnp.concatenate([own_piece[None], others])
        near, away = jnp.split(lax.all_gather(every, "ctx", axis=2, tiled=True), 2, axis=2)
        own_piece, others, own_away = near[0], near[1:], away[0]
        others_away = [away[1:, low:high] for low, high in low_high]

    gathered = []
    for block in columns:
        near = [block] + [dp_send(block, mid_by(step)) for step in range(1, mid_count)]
        gathered.append(near + [dp_send(near_one, swap_core) for near_one in near])
    together = lambda half, dtype: [
        product(half, own_piece, others, own_away, others_away[half], grads, dtype)
        for grads in gathered
    ]
    sent = together(0, jnp.bfloat16)
    others_away[1], _ = lax.optimization_barrier((others_away[1], sent))
    kept = together(1, jnp.float32)
    halves = [
        near + dp_send(far, flip_slow(1)).astype(jnp.float32) for near, far in zip(kept, sent)
    ]
    last = [dp_send(half[:rows].astype(jnp.bfloat16), flip_slow(2)) for half in halves]
    parts = [half[rows:] + final.astype(jnp.float32) for half, final in zip(halves, last)]
    query_parts, _ = lax.optimization_barrier(([outs[0] for outs in attended], kept[0]))
    query_grad = jnp.concatenate(query_parts, axis=1)
    if ctx_count == 2:
        value_rim = jnp.concatenate([outs[5] for outs in attended], axis=1)
        value_rim, _ = lax.optimization_barrier((value_rim, halves[0]))
        returned = lax.ppermute(value_rim, "ctx", [(1, 0)])
        value_own = jnp.concatenate([outs[4] for outs in attended], axis=1)
        value_grad = (value_own.astype(jnp.float32) + returned.astype(jnp.float32)).astype(
            jnp.bfloat16
        )
    if ctx_count == 2:
        parts[-1], value_grad = lax.optimization_barrier((parts[-1], value_grad))
    weight_grad = jnp.concatenate(parts, axis=1)
    return (query_grad[None], key_grad[None], value_grad[None], weight_grad)


def solution(mesh):
    placed = (
        P("dp", "ctx", None),
        P("dp", "ctx", None),
        P("dp", "ctx", None),
        P("dp", "ctx", None),
        P("dp", "ctx", None),
        P("dp", "ctx"),
    )
    return jax.shard_map(
        local,
        mesh=mesh,
        in_specs=placed,
        out_specs=(
            P("dp", "ctx", None),
            P("dp", "ctx", None),
            P("dp", "ctx", None),
            P("dp", "ctx"),
        ),
        check_vma=False,
    )
```

```python
from functools import partial

import jax
import jax.numpy as jnp
from jax import lax
from jax.experimental import pallas as pl
from jax.experimental.pallas import tpu as pltpu
from jax.sharding import PartitionSpec as P

HD = 128
WIN = 1024
CHUNKS = 2
SCORE_FLOOR = -1e30
MIB = 1024 * 1024
SEG_ROWS = 16
SMALL = pl.CostEstimate(flops=1024, bytes_accessed=1024, transcendentals=0)

NT = (((1,), (1,)), ((), ()))
TN = (((0,), (0,)), ((), ()))


def dot_f32(left, right, dims=(((1,), (0,)), ((), ()))):
    return lax.dot_general(left, right, dims, preferred_element_type=jnp.float32)


def shifted(value, axis, steps):
    count = lax.axis_size(axis)
    leading, last = (max(0, -steps), min(count, count - steps))
    return lax.ppermute(value, axis, [(source, source + steps) for source in range(leading, last)])


def attention_kernel(chunk, hops, group, place_ref, *refs):
    segs_ref, query_ref, grad_ref, key_ref, value_ref = refs[:5]
    rim_pairs, rim_segs, refs = refs[5 : 5 + hops], refs[5 + hops : 5 + 2 * hops], refs[5 + 2 * hops :]
    tok = query_ref.shape[0]
    heads = key_ref.shape[1] // HD
    rim = hops * tok
    span = rim + tok
    place = place_ref[0]
    scale = HD**-0.5

    query_segs = segs_ref[:1].astype(jnp.float32)
    key_cols = [
        jnp.transpose(jnp.broadcast_to(ref[...].astype(jnp.float32)[:1], (tok, tok)))
        for ref in (*rim_segs, segs_ref)
    ]
    key_segs = jnp.concatenate(key_cols, axis=0)
    key_at = lax.broadcasted_iota(jnp.int32, (span, tok), 0)
    distance = rim + lax.broadcasted_iota(jnp.int32, (span, tok), 1) - key_at
    allowed = (
        (key_at >= rim - place * tok)
        & (distance >= 0)
        & (distance < WIN)
        & (key_segs == query_segs)
    )
    floor = jnp.where(allowed, 0.0, SCORE_FLOOR)
    floor = jnp.concatenate([floor] * group, axis=1)
    keep = floor == 0.0

    for head in range(heads):
        cols = slice(head * HD, (head + 1) * HD)
        value_cols = slice((heads + head) * HD, (heads + head + 1) * HD)
        q_cols = [slice((head * group + g) * HD, (head * group + g + 1) * HD) for g in range(group)]
        query = jnp.concatenate([query_ref[:, c] for c in q_cols], axis=0)
        grad = jnp.concatenate([grad_ref[:, c] for c in q_cols], axis=0)
        keys = jnp.concatenate([ref[:tok, cols] for ref in rim_pairs] + [key_ref[:, cols]], axis=0)
        values = jnp.concatenate(
            [ref[:tok, value_cols] for ref in rim_pairs] + [value_ref[:, cols]], axis=0
        )
        scores = jnp.where(keep, dot_f32(keys, query, NT) * scale, SCORE_FLOOR)
        weights = jnp.exp(scores - jnp.max(scores, axis=0, keepdims=True))
        probs = weights * (1.0 / jnp.sum(weights, axis=0, keepdims=True))
        probs_low = probs.astype(jnp.bfloat16)
        dprobs = dot_f32(values, grad, NT)
        delta = jnp.sum(probs_low.astype(jnp.float32) * dprobs, axis=0, keepdims=True)
        dscores = (probs * (dprobs - delta)).astype(jnp.bfloat16)
        query_part = (dot_f32(dscores, keys, TN) * scale).astype(jnp.bfloat16)
        key_part = dot_f32(dscores, query) * scale
        value_part = dot_f32(probs_low, grad)
        if hops == 1:
            piece_ref, query_out, sent, addend, key_out, value_out, rim_out = refs
            first = place == 0
            key_rim, key_own = key_part[:tok], key_part[tok:]
            value_rim, value_own = value_part[:tok], value_part[tok:]
            sent[:tok, cols] = jnp.where(first, value_own, key_rim).astype(jnp.bfloat16)
            low = (chunk * heads + head) * tok
            high = min(low + tok, piece_ref.shape[0])
            late = key_own.astype(jnp.bfloat16)
            if low < high:
                part = piece_ref[low:high]
                if high - low < tok:
                    part = jnp.concatenate([part, late[: tok - (high - low)]], axis=0)
                late = jnp.where(first, part, late)
            sent[tok:, cols] = late
            addend[:, cols] = jnp.where(first, key_own, value_rim).astype(jnp.bfloat16)
            key_out[:, cols] = key_own.astype(jnp.bfloat16)
            value_out[:, cols] = value_own.astype(jnp.bfloat16)
            rim_out[:, cols] = value_rim.astype(jnp.bfloat16)
        else:
            query_out = refs[0]
            refs[1][:, cols] = key_part.astype(jnp.bfloat16)
            refs[2][:, cols] = value_part.astype(jnp.bfloat16)
        for g, c in enumerate(q_cols):
            query_out[:, c] = query_part[g * tok : (g + 1) * tok]


def attend(chunk, place, segs, queries, out_grad, keys, values, rim_pairs, rim_segs, piece):
    hops = len(rim_pairs)
    tok = queries.shape[0]
    group = queries.shape[1] // keys.shape[1]
    width = keys.shape[1] // CHUNKS
    span = (hops + 1) * tok
    whole = lambda *shape: pl.BlockSpec(shape, lambda i, *_: (0,) * len(shape))
    part = lambda *shape: pl.BlockSpec(shape, lambda i, *_: (0, chunk))
    seg_row = pl.BlockSpec((SEG_ROWS, tok), lambda i, *_: (tok // SEG_ROWS, 0))
    out_shapes = [(tok, group * width)]
    if hops == 1:
        out_shapes += [(2 * tok, width)] + [(tok, width)] * 4
    else:
        out_shapes += [(span, width)] * 2
    operands = [place, segs, queries, out_grad, keys, values, *rim_pairs, *rim_segs, *piece]
    return pl.pallas_call(
        partial(attention_kernel, chunk, hops, group),
        grid_spec=pltpu.PrefetchScalarGridSpec(
            num_scalar_prefetch=1,
            grid=(1,),
            in_specs=[
                whole(SEG_ROWS, tok),
                part(tok, group * width),
                part(tok, group * width),
                part(tok, width),
                part(tok, width),
            ]
            + [whole(tok, 2 * width)] * hops
            + [seg_row] * hops
            + [whole(*array.shape) for array in piece],
            out_specs=[whole(*shape) for shape in out_shapes],
        ),
        out_shape=[jax.ShapeDtypeStruct(shape, jnp.bfloat16) for shape in out_shapes],
        compiler_params=pltpu.CompilerParams(vmem_limit_bytes=48 * MIB),
        cost_estimate=SMALL,
    )(*operands)


def product_kernel(half, traces, place_ref, own_ref, others_ref, others_away_ref, *refs):
    grad_refs, refs = refs[:traces], refs[traces:]
    others = range(others_ref.shape[0])
    rows, tok = others_away_ref.shape[1:]
    if len(refs) > 2:
        rim_ref, *back_refs = refs[: 1 + CHUNKS]
        refs = refs[1 + CHUNKS :]
        backs = jnp.concatenate([ref[tok:] for ref in back_refs], axis=1)
        blocks = jnp.where(place_ref[0] == 0, rim_ref[...], backs)
        own_away = jnp.concatenate(
            [blocks[:, low : low + HD] for low in range(0, 2 * rows, HD)], axis=0
        )[half * rows : (half + 1) * rows]
    else:
        own_away, refs = refs[0][...], refs[1:]
    (out_ref,) = refs
    grads = jnp.concatenate([ref[...] for ref in grad_refs], axis=0)
    near = [own_ref[...]] + [others_ref[t] for t in others]
    away = [own_away] + [others_away_ref[t] for t in others]
    features = jnp.concatenate([piece for pair in zip(near, away) for piece in pair], axis=1)
    out_ref[...] = dot_f32(features, grads).astype(out_ref.dtype)


def product(half, place, own, others, own_away, others_away, grads, dtype):
    traces, rows, tok = others.shape
    rows //= 2
    width = grads[0].shape[1]
    of_half = lambda array: pl.BlockSpec((rows, array.shape[1]), lambda i, *_: (half, 0))
    whole = lambda array: pl.BlockSpec(array.shape, lambda i, *_: (0,) * array.ndim)
    return pl.pallas_call(
        partial(product_kernel, half, len(grads)),
        grid_spec=pltpu.PrefetchScalarGridSpec(
            num_scalar_prefetch=1,
            grid=(1,),
            in_specs=[
                of_half(own),
                pl.BlockSpec((traces, rows, tok), lambda i, *_: (0, half, 0)),
                whole(others_away),
            ]
            + [whole(piece) for piece in grads]
            + [(whole if len(own_away) > 1 else of_half)(piece) for piece in own_away],
            out_specs=pl.BlockSpec((rows, width), lambda i, *_: (0, 0)),
        ),
        out_shape=jax.ShapeDtypeStruct((rows, width), dtype),
        compiler_params=pltpu.CompilerParams(vmem_limit_bytes=48 * MIB),
        cost_estimate=SMALL,
    )(place, own, others, others_away, *grads, *own_away)


def local(hidden_in, queries, key_states, value_states, out_grad, segment_ids):
    tok = queries.shape[1]
    key_width = key_states.shape[2]
    width = key_width // CHUNKS
    ctx_count = lax.axis_size("ctx")
    hops = min(WIN // tok, ctx_count - 1)
    place = lax.axis_index("ctx")
    first = place == 0
    place_arg = place.astype(jnp.int32).reshape(1)

    dp_count = lax.axis_size("dp")
    slow_count, core_count = 4, 2
    mid_count = dp_count // (slow_count * core_count)
    dp_place = lax.axis_index("dp")
    core_at = dp_place % core_count
    mid_at = dp_place // core_count % mid_count
    slow_at = dp_place // (core_count * mid_count)

    def dp_send(value, move):
        pairs = []
        for source in range(dp_count):
            core = source % core_count
            mid = source // core_count % mid_count
            slow = source // (core_count * mid_count)
            slow, mid, core = move(slow, mid, core)
            pairs.append((source, (slow * mid_count + mid) * core_count + core))
        return lax.ppermute(value, "dp", pairs)

    swap_core = lambda slow, mid, core: (slow, mid, core ^ 1)
    mid_by = lambda step: lambda slow, mid, core: (slow, (mid + step) % mid_count, core)
    flip_slow = lambda bit: lambda slow, mid, core: (slow ^ bit, mid, core)
    swap_ctx = [(c, c ^ 1) for c in range(ctx_count)]

    own_keys, own_values = key_states[0], value_states[0]

    rows = hidden_in.shape[2] // dp_count
    by_feature = hidden_in[0].T.reshape(slow_count, mid_count, core_count, rows, tok)
    by_feature = jnp.stack(
        [lax.dynamic_index_in_dim(by_feature, slow_at ^ turn, 0, False) for turn in (3, 1, 2, 0)]
    )
    of_mid = lambda at: lax.dynamic_index_in_dim(by_feature, at % mid_count, 1, False)
    mids = [of_mid(mid_at)]
    mids += [dp_send(of_mid(mid_at + step), mid_by(step)) for step in range(1, mid_count)]
    share_of = lambda array, core: lax.dynamic_index_in_dim(array, core, -3, False).reshape(
        array.shape[:-4] + (slow_count * rows, tok)
    )
    own_piece = share_of(mids[0], core_at)

    steps = range(hops, 0, -1)
    seg_rows = jnp.broadcast_to(segment_ids.astype(jnp.bfloat16), (SEG_ROWS, tok))
    wide_rows = jnp.pad(seg_rows, ((0, 0), (0, 2 * width - tok)))
    rim_pairs = []
    for chunk in range(CHUNKS):
        cols = slice(chunk * width, (chunk + 1) * width)
        pair = jnp.concatenate([own_keys[:, cols], own_values[:, cols]], axis=1)
        if chunk == 0:
            pair = jnp.concatenate([pair, wide_rows], axis=0)
        if ctx_count == 2 and chunk == CHUNKS - 1:
            back = jnp.pad(own_piece, ((0, 2 * width - own_piece.shape[0]), (0, 0)))
            back = back.reshape(-1, tok, HD).transpose(1, 0, 2).reshape(tok, -1)
            rim_pairs.append([lax.ppermute(jnp.where(first, pair, back), "ctx", swap_ctx)])
        else:
            rim_pairs.append([shifted(pair, "ctx", step) for step in steps])

    half_rows = slow_count // 2 * rows
    low_high = [(0, half_rows), (half_rows, 2 * half_rows)]

    mids = jnp.stack(mids)
    sent_core = share_of(mids, 1 - core_at)
    attended = []
    for chunk in range(CHUNKS):
        if chunk == 1:
            rim_pairs[1], sent_core, _ = lax.optimization_barrier(
                (rim_pairs[1], sent_core, attended[0][1])
            )
        attended.append(
            attend(
                chunk,
                place_arg,
                seg_rows,
                queries[0],
                out_grad[0],
                own_keys,
                own_values,
                rim_pairs[chunk],
                rim_pairs[0],
                [own_piece] if hops == 1 else [],
            )
        )
    kept_core = share_of(mids, core_at)
    other_core = dp_send(sent_core, swap_core)
    others = jnp.concatenate([kept_core[1:], other_core])

    if ctx_count == 2:
        columns, held_back, others_away = [], [], []
        for chunk, (_, sent, addend, key_own, value_own, _) in enumerate(attended):
            arrived = lax.ppermute(sent, "ctx", swap_ctx)
            held_back.append(arrived)
            if chunk == 0:
                arrived, _ = lax.optimization_barrier((arrived, rim_pairs[1:]))
            else:
                arrived, _ = lax.optimization_barrier((arrived, columns[-1]))
            total = (addend.astype(jnp.float32) + arrived[:tok].astype(jnp.float32)).astype(
                jnp.bfloat16
            )
            block = jnp.concatenate(
                [jnp.where(first, total, value_own), jnp.where(first, arrived[tok:], total)], axis=0
            )
            if chunk == 0:
                for low, high in low_high:
                    rest, block = lax.optimization_barrier((others[:, low:high], block))
                    others_away.append(lax.ppermute(rest, "ctx", swap_ctx))
            columns.append(block)
        own_away = [rim_pairs[-1][0], *held_back]
        key_grad = jnp.where(
            first,
            jnp.concatenate([block[:tok] for block in columns], axis=1),
            jnp.concatenate([outs[3] for outs in attended], axis=1),
        )
    else:
        key_rows = jnp.concatenate([outs[1] for outs in attended], axis=1)
        value_rows = jnp.concatenate([outs[2] for outs in attended], axis=1)
        totals = [part[hops * tok :].astype(jnp.float32) for part in (key_rows, value_rows)]
        for step in range(1, hops + 1):
            low = (hops - step) * tok
            totals = [
                total + shifted(part[low : low + tok], "ctx", -step).astype(jnp.float32)
                for total, part in zip(totals, (key_rows, value_rows))
            ]
        key_grad, value_grad = (total.astype(jnp.bfloat16) for total in totals)
        both = lax.all_to_all(
            jnp.concatenate([key_grad, value_grad], axis=1),
            "ctx",
            split_axis=1,
            concat_axis=0,
            tiled=True,
        )
        columns = jnp.split(both, CHUNKS, axis=1)
        every = jnp.concatenate([own_piece[None], others])
        near, away = jnp.split(lax.all_gather(every, "ctx", axis=2, tiled=True), 2, axis=2)
        own_piece, others, own_away = near[0], near[1:], [away[0]]
        others_away = [away[1:, low:high] for low, high in low_high]

    gathered = []
    for block in columns:
        near = [block] + [dp_send(block, mid_by(step)) for step in range(1, mid_count)]
        gathered.append(near + [dp_send(near_one, swap_core) for near_one in near])
    def together(half, dtype):
        ends = (place_arg, own_piece, others, own_away, others_away[half])
        return [product(half, *ends, grads, dtype) for grads in gathered]

    sent = together(0, jnp.bfloat16)
    others_away[1], _ = lax.optimization_barrier((others_away[1], sent))
    kept = together(1, jnp.float32)
    halves = [
        near + dp_send(far, flip_slow(1)).astype(jnp.float32) for near, far in zip(kept, sent)
    ]
    last = [dp_send(half[:rows].astype(jnp.bfloat16), flip_slow(2)) for half in halves]
    parts = [half[rows:] + final.astype(jnp.float32) for half, final in zip(halves, last)]
    query_parts, _ = lax.optimization_barrier(([outs[0] for outs in attended], kept[0]))
    query_grad = jnp.concatenate(query_parts, axis=1)
    if ctx_count == 2:
        value_rims, _ = lax.optimization_barrier(([outs[5] for outs in attended], halves[0]))
        value_rim = jnp.concatenate(value_rims, axis=1)
        returned = lax.ppermute(value_rim, "ctx", [(1, 0)])
        value_own = jnp.concatenate([outs[4] for outs in attended], axis=1)
        value_grad = (value_own.astype(jnp.float32) + returned.astype(jnp.float32)).astype(
            jnp.bfloat16
        )
    weight_grad = jnp.concatenate(parts, axis=1)
    return (query_grad[None], key_grad[None], value_grad[None], weight_grad)


def solution(mesh):
    placed = (
        P("dp", "ctx", None),
        P("dp", "ctx", None),
        P("dp", "ctx", None),
        P("dp", "ctx", None),
        P("dp", "ctx", None),
        P("dp", "ctx"),
    )
    return jax.shard_map(
        local,
        mesh=mesh,
        in_specs=placed,
        out_specs=(
            P("dp", "ctx", None),
            P("dp", "ctx", None),
            P("dp", "ctx", None),
            P("dp", "ctx"),
        ),
        check_vma=False,
    )
```

```python
from functools import partial

import jax
import jax.numpy as jnp
from jax import lax
from jax.experimental import pallas as pl
from jax.experimental.pallas import tpu as pltpu
from jax.sharding import PartitionSpec as P

HD = 128
WIN = 1024
CHUNKS = 2
SCORE_FLOOR = -1e30
MIB = 1024 * 1024
SEG_ROWS = 16
SMALL = pl.CostEstimate(flops=1024, bytes_accessed=1024, transcendentals=0)

NT = (((1,), (1,)), ((), ()))
TN = (((0,), (0,)), ((), ()))


def dot_f32(left, right, dims=(((1,), (0,)), ((), ()))):
    return lax.dot_general(left, right, dims, preferred_element_type=jnp.float32)


def shifted(value, axis, steps):
    count = lax.axis_size(axis)
    leading, last = (max(0, -steps), min(count, count - steps))
    return lax.ppermute(value, axis, [(source, source + steps) for source in range(leading, last)])


def attention_kernel(chunk, hops, group, place_ref, *refs):
    segs_ref, query_ref, grad_ref, key_ref, value_ref = refs[:5]
    rim_pairs, rim_segs, refs = refs[5 : 5 + hops], refs[5 + hops : 5 + 2 * hops], refs[5 + 2 * hops :]
    tok = query_ref.shape[0]
    heads = key_ref.shape[1] // HD
    rim = hops * tok
    span = rim + tok
    place = place_ref[0]
    scale = HD**-0.5

    query_segs = segs_ref[:1].astype(jnp.float32)
    key_cols = [
        jnp.transpose(jnp.broadcast_to(ref[...].astype(jnp.float32)[:1], (tok, tok)))
        for ref in (*rim_segs, segs_ref)
    ]
    key_segs = jnp.concatenate(key_cols, axis=0)
    key_at = lax.broadcasted_iota(jnp.int32, (span, tok), 0)
    distance = rim + lax.broadcasted_iota(jnp.int32, (span, tok), 1) - key_at
    allowed = (
        (key_at >= rim - place * tok)
        & (distance >= 0)
        & (distance < WIN)
        & (key_segs == query_segs)
    )
    floor = jnp.where(allowed, 0.0, SCORE_FLOOR)
    floor = jnp.concatenate([floor] * group, axis=1)
    keep = floor == 0.0

    for head in range(heads):
        cols = slice(head * HD, (head + 1) * HD)
        value_cols = slice((heads + head) * HD, (heads + head + 1) * HD)
        q_cols = [slice((head * group + g) * HD, (head * group + g + 1) * HD) for g in range(group)]
        query = jnp.concatenate([query_ref[:, c] for c in q_cols], axis=0)
        grad = jnp.concatenate([grad_ref[:, c] for c in q_cols], axis=0)
        keys = jnp.concatenate([ref[:tok, cols] for ref in rim_pairs] + [key_ref[:, cols]], axis=0)
        values = jnp.concatenate(
            [ref[:tok, value_cols] for ref in rim_pairs] + [value_ref[:, cols]], axis=0
        )
        scores = jnp.where(keep, dot_f32(keys, query, NT) * scale, SCORE_FLOOR)
        weights = jnp.exp(scores - jnp.max(scores, axis=0, keepdims=True))
        probs = weights * (1.0 / jnp.sum(weights, axis=0, keepdims=True))
        probs_low = probs.astype(jnp.bfloat16)
        dprobs = dot_f32(values, grad, NT)
        delta = jnp.sum(probs_low.astype(jnp.float32) * dprobs, axis=0, keepdims=True)
        dscores = (probs * (dprobs - delta)).astype(jnp.bfloat16)
        query_part = (dot_f32(dscores, keys, TN) * scale).astype(jnp.bfloat16)
        key_part = dot_f32(dscores, query) * scale
        value_part = dot_f32(probs_low, grad)
        if hops == 1:
            piece_ref, query_out, sent, addend, key_out, value_out, rim_out = refs
            first = place == 0
            key_rim, key_own = key_part[:tok], key_part[tok:]
            value_rim, value_own = value_part[:tok], value_part[tok:]
            sent[:tok, cols] = jnp.where(first, value_own, key_rim).astype(jnp.bfloat16)
            low = (chunk * heads + head) * tok
            high = min(low + tok, piece_ref.shape[0])
            late = key_own.astype(jnp.bfloat16)
            if low < high:
                part = piece_ref[low:high]
                if high - low < tok:
                    part = jnp.concatenate([part, late[: tok - (high - low)]], axis=0)
                late = jnp.where(first, part, late)
            sent[tok:, cols] = late
            addend[:, cols] = jnp.where(first, key_own, value_rim).astype(jnp.bfloat16)
            key_out[:, cols] = key_own.astype(jnp.bfloat16)
            value_out[:, cols] = value_own.astype(jnp.bfloat16)
            rim_out[:, cols] = value_rim.astype(jnp.bfloat16)
        else:
            query_out = refs[0]
            refs[1][:, cols] = key_part.astype(jnp.bfloat16)
            refs[2][:, cols] = value_part.astype(jnp.bfloat16)
        for g, c in enumerate(q_cols):
            query_out[:, c] = query_part[g * tok : (g + 1) * tok]


def attend(chunk, place, segs, queries, out_grad, keys, values, rim_pairs, rim_segs, piece):
    hops = len(rim_pairs)
    tok = queries.shape[0]
    group = queries.shape[1] // keys.shape[1]
    width = keys.shape[1] // CHUNKS
    span = (hops + 1) * tok
    whole = lambda *shape: pl.BlockSpec(shape, lambda i, *_: (0,) * len(shape))
    part = lambda *shape: pl.BlockSpec(shape, lambda i, *_: (0, chunk))
    seg_row = pl.BlockSpec((SEG_ROWS, tok), lambda i, *_: (tok // SEG_ROWS, 0))
    out_shapes = [(tok, group * width)]
    if hops == 1:
        out_shapes += [(2 * tok, width)] + [(tok, width)] * 4
    else:
        out_shapes += [(span, width)] * 2
    operands = [place, segs, queries, out_grad, keys, values, *rim_pairs, *rim_segs, *piece]
    return pl.pallas_call(
        partial(attention_kernel, chunk, hops, group),
        grid_spec=pltpu.PrefetchScalarGridSpec(
            num_scalar_prefetch=1,
            grid=(1,),
            in_specs=[
                whole(SEG_ROWS, tok),
                part(tok, group * width),
                part(tok, group * width),
                part(tok, width),
                part(tok, width),
            ]
            + [whole(tok, 2 * width)] * hops
            + [seg_row] * hops
            + [whole(*array.shape) for array in piece],
            out_specs=[whole(*shape) for shape in out_shapes],
        ),
        out_shape=[jax.ShapeDtypeStruct(shape, jnp.bfloat16) for shape in out_shapes],
        compiler_params=pltpu.CompilerParams(vmem_limit_bytes=48 * MIB),
        cost_estimate=SMALL,
    )(*operands)


def product_kernel(half, traces, place_ref, own_ref, others_ref, others_away_ref, *refs):
    grad_refs, refs = refs[:traces], refs[traces:]
    others = range(others_ref.shape[0])
    rows, tok = others_away_ref.shape[1:]
    if len(refs) > 2:
        rim_ref, *back_refs = refs[: 1 + CHUNKS]
        refs = refs[1 + CHUNKS :]
        backs = jnp.concatenate([ref[tok:] for ref in back_refs], axis=1)
        blocks = jnp.where(place_ref[0] == 0, rim_ref[...], backs)
        own_away = jnp.concatenate(
            [blocks[:, low : low + HD] for low in range(0, 2 * rows, HD)], axis=0
        )[half * rows : (half + 1) * rows]
    else:
        own_away, refs = refs[0][...], refs[1:]
    (out_ref,) = refs
    grads = jnp.concatenate([ref[...] for ref in grad_refs], axis=0)
    near = [own_ref[...]] + [others_ref[t] for t in others]
    away = [own_away] + [others_away_ref[t] for t in others]
    features = jnp.concatenate([piece for pair in zip(near, away) for piece in pair], axis=1)
    out_ref[...] = dot_f32(features, grads).astype(out_ref.dtype)


def product(half, place, own, others, own_away, others_away, grads, dtype):
    traces, rows, tok = others.shape
    rows //= 2
    width = grads[0].shape[1]
    of_half = lambda array: pl.BlockSpec((rows, array.shape[1]), lambda i, *_: (half, 0))
    whole = lambda array: pl.BlockSpec(array.shape, lambda i, *_: (0,) * array.ndim)
    return pl.pallas_call(
        partial(product_kernel, half, len(grads)),
        grid_spec=pltpu.PrefetchScalarGridSpec(
            num_scalar_prefetch=1,
            grid=(1,),
            in_specs=[
                of_half(own),
                pl.BlockSpec((traces, rows, tok), lambda i, *_: (0, half, 0)),
                pl.BlockSpec((traces, rows, tok), lambda i, *_: (0, half, 0)),
            ]
            + [whole(piece) for piece in grads]
            + [(whole if len(own_away) > 1 else of_half)(piece) for piece in own_away],
            out_specs=pl.BlockSpec((rows, width), lambda i, *_: (0, 0)),
        ),
        out_shape=jax.ShapeDtypeStruct((rows, width), dtype),
        compiler_params=pltpu.CompilerParams(vmem_limit_bytes=48 * MIB),
        cost_estimate=SMALL,
    )(place, own, others, others_away, *grads, *own_away)


def local(hidden_in, queries, key_states, value_states, out_grad, segment_ids):
    tok = queries.shape[1]
    key_width = key_states.shape[2]
    width = key_width // CHUNKS
    ctx_count = lax.axis_size("ctx")
    hops = min(WIN // tok, ctx_count - 1)
    place = lax.axis_index("ctx")
    first = place == 0
    place_arg = place.astype(jnp.int32).reshape(1)

    dp_count = lax.axis_size("dp")
    slow_count, core_count = 4, 2
    mid_count = dp_count // (slow_count * core_count)
    dp_place = lax.axis_index("dp")
    core_at = dp_place % core_count
    mid_at = dp_place // core_count % mid_count
    slow_at = dp_place // (core_count * mid_count)

    def dp_send(value, move):
        pairs = []
        for source in range(dp_count):
            core = source % core_count
            mid = source // core_count % mid_count
            slow = source // (core_count * mid_count)
            slow, mid, core = move(slow, mid, core)
            pairs.append((source, (slow * mid_count + mid) * core_count + core))
        return lax.ppermute(value, "dp", pairs)

    swap_core = lambda slow, mid, core: (slow, mid, core ^ 1)
    mid_by = lambda step: lambda slow, mid, core: (slow, (mid + step) % mid_count, core)
    flip_slow = lambda bit: lambda slow, mid, core: (slow ^ bit, mid, core)
    swap_ctx = [(c, c ^ 1) for c in range(ctx_count)]

    own_keys, own_values = key_states[0], value_states[0]

    rows = hidden_in.shape[2] // dp_count
    by_feature = hidden_in[0].T.reshape(slow_count, mid_count, core_count, rows, tok)
    by_feature = jnp.stack(
        [lax.dynamic_index_in_dim(by_feature, slow_at ^ turn, 0, False) for turn in (3, 1, 2, 0)]
    )
    of_mid = lambda at: lax.dynamic_index_in_dim(by_feature, at % mid_count, 1, False)
    mids = [of_mid(mid_at)]
    mids += [dp_send(of_mid(mid_at + step), mid_by(step)) for step in range(1, mid_count)]
    share_of = lambda array, core: lax.dynamic_index_in_dim(array, core, -3, False).reshape(
        array.shape[:-4] + (slow_count * rows, tok)
    )
    own_piece = share_of(mids[0], core_at)

    steps = range(hops, 0, -1)
    seg_rows = jnp.broadcast_to(segment_ids.astype(jnp.bfloat16), (SEG_ROWS, tok))
    wide_rows = jnp.pad(seg_rows, ((0, 0), (0, 2 * width - tok)))
    rim_pairs = []
    for chunk in range(CHUNKS):
        cols = slice(chunk * width, (chunk + 1) * width)
        pair = jnp.concatenate([own_keys[:, cols], own_values[:, cols]], axis=1)
        if chunk == 0:
            pair = jnp.concatenate([pair, wide_rows], axis=0)
        if ctx_count == 2 and chunk == CHUNKS - 1:
            back = jnp.pad(own_piece, ((0, 2 * width - own_piece.shape[0]), (0, 0)))
            back = back.reshape(-1, tok, HD).transpose(1, 0, 2).reshape(tok, -1)
            rim_pairs.append([lax.ppermute(jnp.where(first, pair, back), "ctx", swap_ctx)])
        else:
            rim_pairs.append([shifted(pair, "ctx", step) for step in steps])


    mids = jnp.stack(mids)
    sent_core = share_of(mids, 1 - core_at)
    attended = []
    for chunk in range(CHUNKS):
        if chunk == 1:
            rim_pairs[1], sent_core, _ = lax.optimization_barrier(
                (rim_pairs[1], sent_core, attended[0][1])
            )
        attended.append(
            attend(
                chunk,
                place_arg,
                seg_rows,
                queries[0],
                out_grad[0],
                own_keys,
                own_values,
                rim_pairs[chunk],
                rim_pairs[0],
                [own_piece] if hops == 1 else [],
            )
        )
    kept_core = share_of(mids, core_at)
    other_core = dp_send(sent_core, swap_core)
    others = jnp.concatenate([kept_core[1:], other_core])

    if ctx_count == 2:
        columns, held_back = [], []
        for chunk, (_, sent, addend, key_own, value_own, _) in enumerate(attended):
            arrived = lax.ppermute(sent, "ctx", swap_ctx)
            held_back.append(arrived)
            if chunk == 0:
                arrived, _ = lax.optimization_barrier((arrived, rim_pairs[1:]))
            else:
                arrived, _ = lax.optimization_barrier((arrived, columns[-1]))
            total = (addend.astype(jnp.float32) + arrived[:tok].astype(jnp.float32)).astype(
                jnp.bfloat16
            )
            block = jnp.concatenate(
                [jnp.where(first, total, value_own), jnp.where(first, arrived[tok:], total)], axis=0
            )
            if chunk == 0:
                rest, block = lax.optimization_barrier((others, block))
                others_away = lax.ppermute(rest, "ctx", swap_ctx)
            columns.append(block)
        own_away = [rim_pairs[-1][0], *held_back]
        key_grad = jnp.where(
            first,
            jnp.concatenate([block[:tok] for block in columns], axis=1),
            jnp.concatenate([outs[3] for outs in attended], axis=1),
        )
    else:
        key_rows = jnp.concatenate([outs[1] for outs in attended], axis=1)
        value_rows = jnp.concatenate([outs[2] for outs in attended], axis=1)
        totals = [part[hops * tok :].astype(jnp.float32) for part in (key_rows, value_rows)]
        for step in range(1, hops + 1):
            low = (hops - step) * tok
            totals = [
                total + shifted(part[low : low + tok], "ctx", -step).astype(jnp.float32)
                for total, part in zip(totals, (key_rows, value_rows))
            ]
        key_grad, value_grad = (total.astype(jnp.bfloat16) for total in totals)
        both = lax.all_to_all(
            jnp.concatenate([key_grad, value_grad], axis=1),
            "ctx",
            split_axis=1,
            concat_axis=0,
            tiled=True,
        )
        columns = jnp.split(both, CHUNKS, axis=1)
        every = jnp.concatenate([own_piece[None], others])
        near, away = jnp.split(lax.all_gather(every, "ctx", axis=2, tiled=True), 2, axis=2)
        own_piece, others, own_away = near[0], near[1:], [away[0]]
        others_away = away[1:]

    gathered = []
    for block in columns:
        near = [block] + [dp_send(block, mid_by(step)) for step in range(1, mid_count)]
        gathered.append(near + [dp_send(near_one, swap_core) for near_one in near])
    def together(half, dtype):
        ends = (place_arg, own_piece, others, own_away, others_away)
        return [product(half, *ends, grads, dtype) for grads in gathered]

    sent = together(0, jnp.bfloat16)
    others_away, _ = lax.optimization_barrier((others_away, sent))
    kept = together(1, jnp.float32)
    halves = [
        near + dp_send(far, flip_slow(1)).astype(jnp.float32) for near, far in zip(kept, sent)
    ]
    last = [dp_send(half[:rows].astype(jnp.bfloat16), flip_slow(2)) for half in halves]
    parts = [half[rows:] + final.astype(jnp.float32) for half, final in zip(halves, last)]
    query_parts, _ = lax.optimization_barrier(([outs[0] for outs in attended], kept[0]))
    query_grad = jnp.concatenate(query_parts, axis=1)
    if ctx_count == 2:
        value_rims, _ = lax.optimization_barrier(([outs[5] for outs in attended], halves[0]))
        value_rim = jnp.concatenate(value_rims, axis=1)
        returned = lax.ppermute(value_rim, "ctx", [(1, 0)])
        value_own = jnp.concatenate([outs[4] for outs in attended], axis=1)
        value_grad = (value_own.astype(jnp.float32) + returned.astype(jnp.float32)).astype(
            jnp.bfloat16
        )
    weight_grad = jnp.concatenate(parts, axis=1)
    return (query_grad[None], key_grad[None], value_grad[None], weight_grad)


def solution(mesh):
    placed = (
        P("dp", "ctx", None),
        P("dp", "ctx", None),
        P("dp", "ctx", None),
        P("dp", "ctx", None),
        P("dp", "ctx", None),
        P("dp", "ctx"),
    )
    return jax.shard_map(
        local,
        mesh=mesh,
        in_specs=placed,
        out_specs=(
            P("dp", "ctx", None),
            P("dp", "ctx", None),
            P("dp", "ctx", None),
            P("dp", "ctx"),
        ),
        check_vma=False,
    )
```

```python
from functools import partial

import jax
import jax.numpy as jnp
from jax import lax
from jax.experimental import pallas as pl
from jax.experimental.pallas import tpu as pltpu
from jax.sharding import PartitionSpec as P

HD = 128
WIN = 1024
CHUNKS = 2
SCORE_FLOOR = -1e30
MIB = 1024 * 1024
SEG_ROWS = 16
SMALL = pl.CostEstimate(flops=1024, bytes_accessed=1024, transcendentals=0)

NT = (((1,), (1,)), ((), ()))
TN = (((0,), (0,)), ((), ()))


def dot_f32(left, right, dims=(((1,), (0,)), ((), ()))):
    return lax.dot_general(left, right, dims, preferred_element_type=jnp.float32)


def shifted(value, axis, steps):
    count = lax.axis_size(axis)
    leading, last = (max(0, -steps), min(count, count - steps))
    return lax.ppermute(value, axis, [(source, source + steps) for source in range(leading, last)])


def attention_kernel(chunk, hops, group, place_ref, *refs):
    segs_ref, query_ref, grad_ref, key_ref, value_ref = refs[:5]
    rim_pairs, rim_segs, refs = refs[5 : 5 + hops], refs[5 + hops : 5 + 2 * hops], refs[5 + 2 * hops :]
    tok = query_ref.shape[0]
    heads = key_ref.shape[1] // HD
    rim = hops * tok
    span = rim + tok
    place = place_ref[0]
    scale = HD**-0.5

    query_segs = segs_ref[:1].astype(jnp.float32)
    key_cols = [
        jnp.transpose(jnp.broadcast_to(ref[...].astype(jnp.float32)[:1], (tok, tok)))
        for ref in (*rim_segs, segs_ref)
    ]
    key_segs = jnp.concatenate(key_cols, axis=0)
    key_at = lax.broadcasted_iota(jnp.int32, (span, tok), 0)
    distance = rim + lax.broadcasted_iota(jnp.int32, (span, tok), 1) - key_at
    allowed = (
        (key_at >= rim - place * tok)
        & (distance >= 0)
        & (distance < WIN)
        & (key_segs == query_segs)
    )
    floor = jnp.where(allowed, 0.0, SCORE_FLOOR)
    floor = jnp.concatenate([floor] * group, axis=1)
    keep = floor == 0.0

    for head in range(heads):
        cols = slice(head * HD, (head + 1) * HD)
        value_cols = slice((heads + head) * HD, (heads + head + 1) * HD)
        q_cols = [slice((head * group + g) * HD, (head * group + g + 1) * HD) for g in range(group)]
        query = jnp.concatenate([query_ref[:, c] for c in q_cols], axis=0)
        grad = jnp.concatenate([grad_ref[:, c] for c in q_cols], axis=0)
        keys = jnp.concatenate([ref[:tok, cols] for ref in rim_pairs] + [key_ref[:, cols]], axis=0)
        values = jnp.concatenate(
            [ref[:tok, value_cols] for ref in rim_pairs] + [value_ref[:, cols]], axis=0
        )
        scores = jnp.where(keep, dot_f32(keys, query, NT) * scale, SCORE_FLOOR)
        weights = jnp.exp(scores - jnp.max(scores, axis=0, keepdims=True))
        probs = weights * (1.0 / jnp.sum(weights, axis=0, keepdims=True))
        probs_low = probs.astype(jnp.bfloat16)
        dprobs = dot_f32(values, grad, NT)
        delta = jnp.sum(probs_low.astype(jnp.float32) * dprobs, axis=0, keepdims=True)
        dscores = (probs * (dprobs - delta)).astype(jnp.bfloat16)
        query_part = (dot_f32(dscores, keys, TN) * scale).astype(jnp.bfloat16)
        key_part = dot_f32(dscores, query) * scale
        value_part = dot_f32(probs_low, grad)
        if hops == 1:
            piece_ref, query_out, sent, addend, key_out, value_out, rim_out = refs
            first = place == 0
            key_rim, key_own = key_part[:tok], key_part[tok:]
            value_rim, value_own = value_part[:tok], value_part[tok:]
            sent[:tok, cols] = jnp.where(first, value_own, key_rim).astype(jnp.bfloat16)
            low = (chunk * heads + head) * tok
            high = min(low + tok, piece_ref.shape[0])
            late = key_own.astype(jnp.bfloat16)
            if low < high:
                part = piece_ref[low:high]
                if high - low < tok:
                    part = jnp.concatenate([part, late[: tok - (high - low)]], axis=0)
                late = jnp.where(first, part, late)
            sent[tok:, cols] = late
            addend[:, cols] = jnp.where(first, key_own, value_rim).astype(jnp.bfloat16)
            key_out[:, cols] = key_own.astype(jnp.bfloat16)
            value_out[:, cols] = value_own.astype(jnp.bfloat16)
            rim_out[:, cols] = value_rim.astype(jnp.bfloat16)
        else:
            query_out = refs[0]
            refs[1][:, cols] = key_part.astype(jnp.bfloat16)
            refs[2][:, cols] = value_part.astype(jnp.bfloat16)
        for g, c in enumerate(q_cols):
            query_out[:, c] = query_part[g * tok : (g + 1) * tok]


def attend(chunk, place, segs, queries, out_grad, keys, values, rim_pairs, rim_segs, piece):
    hops = len(rim_pairs)
    tok = queries.shape[0]
    group = queries.shape[1] // keys.shape[1]
    width = keys.shape[1] // CHUNKS
    span = (hops + 1) * tok
    whole = lambda *shape: pl.BlockSpec(shape, lambda i, *_: (0,) * len(shape))
    part = lambda *shape: pl.BlockSpec(shape, lambda i, *_: (0, chunk))
    seg_row = pl.BlockSpec((SEG_ROWS, tok), lambda i, *_: (tok // SEG_ROWS, 0))
    out_shapes = [(tok, group * width)]
    if hops == 1:
        out_shapes += [(2 * tok, width)] + [(tok, width)] * 4
    else:
        out_shapes += [(span, width)] * 2
    operands = [place, segs, queries, out_grad, keys, values, *rim_pairs, *rim_segs, *piece]
    return pl.pallas_call(
        partial(attention_kernel, chunk, hops, group),
        grid_spec=pltpu.PrefetchScalarGridSpec(
            num_scalar_prefetch=1,
            grid=(1,),
            in_specs=[
                whole(SEG_ROWS, tok),
                part(tok, group * width),
                part(tok, group * width),
                part(tok, width),
                part(tok, width),
            ]
            + [whole(tok, 2 * width)] * hops
            + [seg_row] * hops
            + [whole(*array.shape) for array in piece],
            out_specs=[whole(*shape) for shape in out_shapes],
        ),
        out_shape=[jax.ShapeDtypeStruct(shape, jnp.bfloat16) for shape in out_shapes],
        compiler_params=pltpu.CompilerParams(vmem_limit_bytes=24 * MIB),
        cost_estimate=SMALL,
    )(*operands)


def product_kernel(half, traces, place_ref, own_ref, others_ref, others_away_ref, *refs):
    grad_refs, refs = refs[:traces], refs[traces:]
    others = range(others_ref.shape[0])
    rows, tok = others_away_ref.shape[1:]
    if len(refs) > 2:
        rim_ref, *back_refs = refs[: 1 + CHUNKS]
        refs = refs[1 + CHUNKS :]
        backs = jnp.concatenate([ref[tok:] for ref in back_refs], axis=1)
        blocks = jnp.where(place_ref[0] == 0, rim_ref[...], backs)
        own_away = jnp.concatenate(
            [blocks[:, low : low + HD] for low in range(0, 2 * rows, HD)], axis=0
        )[half * rows : (half + 1) * rows]
    else:
        own_away, refs = refs[0][...], refs[1:]
    (out_ref,) = refs
    grads = jnp.concatenate([ref[...] for ref in grad_refs], axis=0)
    near = [own_ref[...]] + [others_ref[t] for t in others]
    away = [own_away] + [others_away_ref[t] for t in others]
    features = jnp.concatenate([piece for pair in zip(near, away) for piece in pair], axis=1)
    out_ref[...] = dot_f32(features, grads).astype(out_ref.dtype)


def product(half, place, own, others, own_away, others_away, grads, dtype):
    traces, rows, tok = others.shape
    rows //= 2
    width = grads[0].shape[1]
    of_half = lambda array: pl.BlockSpec((rows, array.shape[1]), lambda i, *_: (half, 0))
    whole = lambda array: pl.BlockSpec(array.shape, lambda i, *_: (0,) * array.ndim)
    return pl.pallas_call(
        partial(product_kernel, half, len(grads)),
        grid_spec=pltpu.PrefetchScalarGridSpec(
            num_scalar_prefetch=1,
            grid=(1,),
            in_specs=[
                of_half(own),
                pl.BlockSpec((traces, rows, tok), lambda i, *_: (0, half, 0)),
                pl.BlockSpec((traces, rows, tok), lambda i, *_: (0, half, 0)),
            ]
            + [whole(piece) for piece in grads]
            + [(whole if len(own_away) > 1 else of_half)(piece) for piece in own_away],
            out_specs=pl.BlockSpec((rows, width), lambda i, *_: (0, 0)),
        ),
        out_shape=jax.ShapeDtypeStruct((rows, width), dtype),
        compiler_params=pltpu.CompilerParams(vmem_limit_bytes=20 * MIB),
        cost_estimate=SMALL,
    )(place, own, others, others_away, *grads, *own_away)


def local(hidden_in, queries, key_states, value_states, out_grad, segment_ids):
    tok = queries.shape[1]
    key_width = key_states.shape[2]
    width = key_width // CHUNKS
    ctx_count = lax.axis_size("ctx")
    hops = min(WIN // tok, ctx_count - 1)
    place = lax.axis_index("ctx")
    first = place == 0
    place_arg = place.astype(jnp.int32).reshape(1)

    dp_count = lax.axis_size("dp")
    slow_count, core_count = 4, 2
    mid_count = dp_count // (slow_count * core_count)
    dp_place = lax.axis_index("dp")
    core_at = dp_place % core_count
    mid_at = dp_place // core_count % mid_count
    slow_at = dp_place // (core_count * mid_count)

    def dp_send(value, move):
        pairs = []
        for source in range(dp_count):
            core = source % core_count
            mid = source // core_count % mid_count
            slow = source // (core_count * mid_count)
            slow, mid, core = move(slow, mid, core)
            pairs.append((source, (slow * mid_count + mid) * core_count + core))
        return lax.ppermute(value, "dp", pairs)

    swap_core = lambda slow, mid, core: (slow, mid, core ^ 1)
    mid_by = lambda step: lambda slow, mid, core: (slow, (mid + step) % mid_count, core)
    flip_slow = lambda bit: lambda slow, mid, core: (slow ^ bit, mid, core)
    swap_ctx = [(c, c ^ 1) for c in range(ctx_count)]

    own_keys, own_values = key_states[0], value_states[0]

    rows = hidden_in.shape[2] // dp_count
    by_feature = hidden_in[0].T.reshape(slow_count, mid_count, core_count, rows, tok)
    by_feature = jnp.stack(
        [lax.dynamic_index_in_dim(by_feature, slow_at ^ turn, 0, False) for turn in (3, 1, 2, 0)]
    )
    of_mid = lambda at: lax.dynamic_index_in_dim(by_feature, at % mid_count, 1, False)
    mids = [of_mid(mid_at)]
    mids += [dp_send(of_mid(mid_at + step), mid_by(step)) for step in range(1, mid_count)]
    share_of = lambda array, core: lax.dynamic_index_in_dim(array, core, -3, False).reshape(
        array.shape[:-4] + (slow_count * rows, tok)
    )
    own_piece = share_of(mids[0], core_at)

    steps = range(hops, 0, -1)
    seg_rows = jnp.broadcast_to(segment_ids.astype(jnp.bfloat16), (SEG_ROWS, tok))
    wide_rows = jnp.pad(seg_rows, ((0, 0), (0, 2 * width - tok)))
    rim_pairs = []
    for chunk in range(CHUNKS):
        cols = slice(chunk * width, (chunk + 1) * width)
        pair = jnp.concatenate([own_keys[:, cols], own_values[:, cols]], axis=1)
        if chunk == 0:
            pair = jnp.concatenate([pair, wide_rows], axis=0)
        if ctx_count == 2 and chunk == CHUNKS - 1:
            back = jnp.pad(own_piece, ((0, 2 * width - own_piece.shape[0]), (0, 0)))
            back = back.reshape(-1, tok, HD).transpose(1, 0, 2).reshape(tok, -1)
            rim_pairs.append([lax.ppermute(jnp.where(first, pair, back), "ctx", swap_ctx)])
        else:
            rim_pairs.append([shifted(pair, "ctx", step) for step in steps])


    mids = jnp.stack(mids)
    sent_core = share_of(mids, 1 - core_at)
    attended = []
    for chunk in range(CHUNKS):
        if chunk == 1:
            rim_pairs[1], sent_core, _ = lax.optimization_barrier(
                (rim_pairs[1], sent_core, attended[0][1])
            )
        attended.append(
            attend(
                chunk,
                place_arg,
                seg_rows,
                queries[0],
                out_grad[0],
                own_keys,
                own_values,
                rim_pairs[chunk],
                rim_pairs[0],
                [own_piece] if hops == 1 else [],
            )
        )
    kept_core = share_of(mids, core_at)
    other_core = dp_send(sent_core, swap_core)
    others = jnp.concatenate([kept_core[1:], other_core])

    if ctx_count == 2:
        columns, held_back = [], []
        for chunk, (_, sent, addend, key_own, value_own, _) in enumerate(attended):
            arrived = lax.ppermute(sent, "ctx", swap_ctx)
            held_back.append(arrived)
            if chunk == 0:
                arrived, _ = lax.optimization_barrier((arrived, rim_pairs[1:]))
            else:
                arrived, _ = lax.optimization_barrier((arrived, columns[-1]))
            total = (addend.astype(jnp.float32) + arrived[:tok].astype(jnp.float32)).astype(
                jnp.bfloat16
            )
            block = jnp.concatenate(
                [jnp.where(first, total, value_own), jnp.where(first, arrived[tok:], total)], axis=0
            )
            if chunk == 0:
                rest, block = lax.optimization_barrier((others, block))
                others_away = lax.ppermute(rest, "ctx", swap_ctx)
            columns.append(block)
        own_away = [rim_pairs[-1][0], *held_back]
        key_grad = jnp.where(
            first,
            jnp.concatenate([block[:tok] for block in columns], axis=1),
            jnp.concatenate([outs[3] for outs in attended], axis=1),
        )
    else:
        key_rows = jnp.concatenate([outs[1] for outs in attended], axis=1)
        value_rows = jnp.concatenate([outs[2] for outs in attended], axis=1)
        totals = [part[hops * tok :].astype(jnp.float32) for part in (key_rows, value_rows)]
        for step in range(1, hops + 1):
            low = (hops - step) * tok
            totals = [
                total + shifted(part[low : low + tok], "ctx", -step).astype(jnp.float32)
                for total, part in zip(totals, (key_rows, value_rows))
            ]
        key_grad, value_grad = (total.astype(jnp.bfloat16) for total in totals)
        both = lax.all_to_all(
            jnp.concatenate([key_grad, value_grad], axis=1),
            "ctx",
            split_axis=1,
            concat_axis=0,
            tiled=True,
        )
        columns = jnp.split(both, CHUNKS, axis=1)
        every = jnp.concatenate([own_piece[None], others])
        near, away = jnp.split(lax.all_gather(every, "ctx", axis=2, tiled=True), 2, axis=2)
        own_piece, others, own_away = near[0], near[1:], [away[0]]
        others_away = away[1:]

    gathered = []
    for block in columns:
        near = [block] + [dp_send(block, mid_by(step)) for step in range(1, mid_count)]
        gathered.append(near + [dp_send(near_one, swap_core) for near_one in near])
    def together(half, dtype):
        ends = (place_arg, own_piece, others, own_away, others_away)
        return [product(half, *ends, grads, dtype) for grads in gathered]

    sent = together(0, jnp.bfloat16)
    others_away, _ = lax.optimization_barrier((others_away, sent))
    kept = together(1, jnp.float32)
    halves = [
        near + dp_send(far, flip_slow(1)).astype(jnp.float32) for near, far in zip(kept, sent)
    ]
    last = [dp_send(half[:rows].astype(jnp.bfloat16), flip_slow(2)) for half in halves]
    parts = [half[rows:] + final.astype(jnp.float32) for half, final in zip(halves, last)]
    query_parts, _ = lax.optimization_barrier(([outs[0] for outs in attended], kept[0]))
    query_grad = jnp.concatenate(query_parts, axis=1)
    if ctx_count == 2:
        value_rims, _ = lax.optimization_barrier(([outs[5] for outs in attended], halves[0]))
        value_rim = jnp.concatenate(value_rims, axis=1)
        returned = lax.ppermute(value_rim, "ctx", [(1, 0)])
        value_own = jnp.concatenate([outs[4] for outs in attended], axis=1)
        value_grad = (value_own.astype(jnp.float32) + returned.astype(jnp.float32)).astype(
            jnp.bfloat16
        )
    weight_grad = jnp.concatenate(parts, axis=1)
    return (query_grad[None], key_grad[None], value_grad[None], weight_grad)


def solution(mesh):
    placed = (
        P("dp", "ctx", None),
        P("dp", "ctx", None),
        P("dp", "ctx", None),
        P("dp", "ctx", None),
        P("dp", "ctx", None),
        P("dp", "ctx"),
    )
    return jax.shard_map(
        local,
        mesh=mesh,
        in_specs=placed,
        out_specs=(
            P("dp", "ctx", None),
            P("dp", "ctx", None),
            P("dp", "ctx", None),
            P("dp", "ctx"),
        ),
        check_vma=False,
    )
```
